512 devices in a mesh: replica: 32 (over y_hi, z, core), expert: 16 (over x, y_lo).
Axes of the slice: x: 4, y: 8 (y_hi: 2, y_lo: 4; y = y_hi * 4 + y_lo), z: 8, core: 2. Of those that a mesh axis runs over, the one named last changes fastest.
Arguments:
- tokens: bfloat16 [65536, 1792], P(('replica', 'expert')), may hold values from -6 to 6
- cotangent: bfloat16 [65536, 1792], P(('replica', 'expert')), may hold values from -0.71875 to 0.71875
- expert_ids: int32 [65536, 1], P(('replica', 'expert')), may hold values from 0 to 1; in each aligned block of 128 rows (0 to 127, 128 to 255, ...) at most 96 rows name the same one
- gate_values: bfloat16 [65536, 1], P(('replica', 'expert')), may hold values from 0.049804688 to 1
- w_gate: bfloat16 [32, 1792, 4096], P('replica', None, 'expert'), may hold values from -0.125 to 0.125
- w_up: bfloat16 [32, 1792, 4096], P('replica', None, 'expert'), may hold values from -0.125 to 0.125
- w_down: bfloat16 [32, 4096, 1792], P('replica', 'expert'), may hold values from -6 to 6
- anchor: float32 [16, 256, 1792], P('expert', 'replica'), may hold values from -6 to 6
- momentum: float32 [16, 256, 1792], P('expert', 'replica'), may hold values from -3 to 3
Outputs:
- gate_grad: float32 [65536, 1], P(('replica', 'expert'))
- new_frag: bfloat16 [32, 16, 256, 1792], P('replica', 'expert')
- new_anchor: float32 [16, 256, 1792], P('expert', 'replica')
- new_momentum: float32 [16, 256, 1792], P('expert', 'replica')
The draws below stay inside these ranges and needn't reach their ends.
Inputs may be any that keep to these rules, and one draw needn't show every extreme that they name: `expert_ids`: each row names one expert. In the rows of one device, no expert is named by more than 96 rows, a bound that some block reaches.
All inputs are finite; a program needn't handle non-finite values.
Results may differ from the reference program's by a relative error of at most 0.015.
Values may be sent and summed in bfloat16 or wider, within the bound.
A program may use at most 128 MiB of HBM per device.

```python
import math
import jax
import jax.numpy as jnp
import numpy as np
from jax import lax

D = 1792
HID = 2048
EXPERTS = 2
TOPK = 1
TOK_DEV = 128
HID_DEV = 256
CAP = 96
TOKENS = 65536
N_REPLICA = 32
N_EXPERT = 16


def levels(rng, extent, shards, low, largest):
    loudness, own = 1.0, jax.random.fold_in(rng, 6)
    for axis_at, blocks in shards:
        draws = jnp.exp(jax.random.uniform(jax.random.fold_in(own, axis_at), (blocks,), jnp.float32, low / len(shards), largest / len(shards)))
        loudness = loudness * jnp.repeat(draws, extent[axis_at] // blocks).reshape([-1 if axis == axis_at else 1 for axis in range(len(extent))])
    return loudness


def assign_block(rng, own, number, rows, number_of, top, limit, slope):
    sequence = jax.random.permutation(rng, number_of)
    crowded, usual = shares(number_of, rows * top, limit, slope, True), shares(number_of, rows * top, limit, slope, False)
    places = jnp.arange(number_of)

    def named(sizes, offset_by):
        used = int((sizes > 0).sum())
        fixed = max(1, used // 4)
        passed = fixed + (places - fixed + offset_by * (used - fixed)) % max(1, number_of - fixed)
        return jnp.zeros((number_of,), jnp.int32).at[sequence[jnp.where(places < fixed, places, passed)]].set(jnp.asarray(sizes, jnp.int32))

    sizes = jnp.where(number % 4 == 0, named(crowded, number // 4), named(usual, number - number // 4 - 1))
    mixed = jax.random.permutation(jax.random.fold_in(own, 3), number_of)
    giver, receiver = mixed[0:number_of // 2 * 2:2], mixed[1:number_of // 2 * 2:2]
    room = jnp.minimum(sizes[giver] - 1, limit - sizes[receiver]) // 2
    room = jnp.where((giver == sequence[0]) | (receiver == sequence[0]) | (sizes[receiver] == 0), 0, jnp.maximum(room, 0))
    passed = jax.random.randint(jax.random.fold_in(own, 4), (number_of // 2,), 0, 1 << 20) % (room + 1)
    sizes = sizes.at[giver].add(-passed).at[receiver].add(passed)
    items = jnp.searchsorted(jnp.cumsum(sizes), jnp.arange(rows * top), side="right").astype(jnp.int32)
    grid = items.reshape(top, rows).T
    grid = grid[jax.random.permutation(jax.random.fold_in(own, 1), rows)]
    offset_by = jax.random.randint(jax.random.fold_in(own, 2), (rows, 1), 0, top)
    return jnp.take_along_axis(grid, (jnp.arange(top)[None, :] + offset_by) % top, axis=1)


def shares(amount, total, most, slope, full):
    loads = [(1 << 20) // math.isqrt(standing ** slope) + 1 for standing in range(1, amount + 1)]
    largest = most if full else min(most, max(-(-total // amount), total * loads[0] // sum(loads)))
    least = 1 if total - largest >= amount - 1 else 0
    given, rest = [largest] + [least] * (amount - 1), total - largest - least * (amount - 1)
    while rest > 0:
        movable = [i for i in range(1, amount) if given[i] < largest] or [i for i in range(1, amount) if given[i] < most]
        whole, budget = sum([loads[i] for i in movable]), rest
        for i in movable:
            extra = min(most - given[i], max(1, budget * loads[i] // whole), rest)
            given[i] = given[i] + extra
            rest = rest - extra
    return np.array(given)


def gaussian(rng, extent, width, bound, shards=(), held_as=jnp.bfloat16):
    drawn = jax.random.normal(rng, extent, jnp.float32) * width
    if len(shards) > 0:
        drawn = levels(rng, extent, shards, -0.22, 0.18) * drawn
    return jnp.clip(drawn, min=-bound, max=bound).astype(held_as)


def setup_inputs(seed: int = 0) -> dict:
    splits = jax.random.split(jax.random.key(seed), 10)
    tokens = gaussian(splits[0], (TOKENS, D), 1.0, 6.0, ((0, 512),))
    cotangent = gaussian(splits[1], (TOKENS, D), 0.12, 0.71875, ((0, 512),))
    expert_ids_keys = jax.random.split(jax.random.fold_in(splits[2], 1), TOKENS // TOK_DEV)
    expert_ids_turns = jax.random.permutation(jax.random.fold_in(splits[2], 3), TOKENS // TOK_DEV)
    expert_ids = jax.vmap(lambda own, number: assign_block(jax.random.fold_in(splits[2], 2), own, number, TOK_DEV, EXPERTS, TOPK, CAP, 2))(expert_ids_keys, expert_ids_turns).reshape((TOKENS, TOPK))
    gate_values = jnp.clip(jnp.exp(math.log(1.0) - 2.9996462 * jax.random.uniform(splits[3], (TOKENS, TOPK), jnp.float32) ** levels(splits[3], (TOKENS, TOPK), ((0, 512),), -0.2, 0.2)), 0.049804688, 1.0).astype(jnp.bfloat16)
    w_gate = gaussian(splits[4], (N_REPLICA, D, EXPERTS * HID), D ** -0.5, 0.125, ((0, 32), (2, 16)))
    w_up = gaussian(splits[5], (N_REPLICA, D, EXPERTS * HID), D ** -0.5, 0.125, ((0, 32), (2, 16)))
    w_down = gaussian(splits[6], (N_REPLICA, EXPERTS * HID, D), 1.0, 6.0, ((0, 32), (1, 16)))
    anchor = gaussian(splits[7], (N_EXPERT, HID_DEV, D), 1.0, 6.0, ((0, 16), (1, 32)), jnp.float32)
    momentum = gaussian(splits[8], (N_EXPERT, HID_DEV, D), 0.5, 3.0, ((0, 16), (1, 32)), jnp.float32)
    return {"tokens": tokens, "cotangent": cotangent, "expert_ids": expert_ids, "gate_values": gate_values, "w_gate": w_gate, "w_up": w_up, "w_down": w_down, "anchor": anchor, "momentum": momentum}


outer_rate = 0.7
outer_momentum = 0.9
mix_weight = 0.5
inner_rate = 8.0

def block_slots(block_ids):
    labels = jnp.arange(EXPERTS, dtype=jnp.int32)
    matched = block_ids[:, :, None] == labels[None, None, :]
    hit_count = lax.optimization_barrier(jnp.sum(matched.astype(jnp.int32), axis=1, dtype=jnp.int32))
    before = jnp.cumsum(hit_count, axis=0, dtype=jnp.int32) - hit_count
    return lax.optimization_barrier(jnp.sum(jnp.where(matched, before[:, None, :], 0), axis=2, dtype=jnp.int32))

def expert_work(operands):
    token_rows, cotangent_rows, gate_rows, gate_weights, up_weights, down_weights = operands
    out_scale = 1.0 / math.sqrt(HID)
    gate_value = jnp.dot(token_rows, gate_weights, preferred_element_type=jnp.float32)
    up_value = jnp.dot(token_rows, up_weights, preferred_element_type=jnp.float32)
    activation = (jax.nn.silu(gate_value) * up_value).astype(jnp.bfloat16)
    product = jnp.dot(activation, down_weights, preferred_element_type=jnp.float32)
    slot_grad = out_scale * lax.optimization_barrier(jnp.sum(product * cotangent_rows.astype(jnp.float32), axis=1))
    scaled_cot = (gate_rows.astype(jnp.float32)[:, None] * cotangent_rows.astype(jnp.float32)).astype(jnp.bfloat16)
    down_grad = out_scale * jnp.dot(activation.T, scaled_cot, preferred_element_type=jnp.float32)
    return (slot_grad, down_grad)

def reference(tokens, cotangent, expert_ids, gate_values, w_gate, w_up, w_down, anchor, momentum):
    replica_rows = N_EXPERT * TOK_DEV
    rows_total = EXPERTS * N_EXPERT * CAP

    def replica_step(replica_index):
        row_start = replica_index * replica_rows
        replica_tokens = lax.dynamic_slice_in_dim(tokens, row_start, replica_rows, 0)
        replica_cot = lax.dynamic_slice_in_dim(cotangent, row_start, replica_rows, 0)
        replica_ids = lax.dynamic_slice_in_dim(expert_ids, row_start, replica_rows, 0)
        replica_gates = lax.dynamic_slice_in_dim(gate_values, row_start, replica_rows, 0)
        gate_weights = lax.dynamic_index_in_dim(w_gate, replica_index, 0, keepdims=False)
        up_weights = lax.dynamic_index_in_dim(w_up, replica_index, 0, keepdims=False)
        down_weights = lax.dynamic_index_in_dim(w_down, replica_index, 0, keepdims=False)
        gate_weights = jnp.transpose(gate_weights.reshape(D, EXPERTS, HID), (1, 0, 2))
        up_weights = jnp.transpose(up_weights.reshape(D, EXPERTS, HID), (1, 0, 2))
        down_weights = down_weights.reshape(EXPERTS, HID, D)
        block_ids = replica_ids.reshape(N_EXPERT, TOK_DEV, TOPK)
        slot_index = jax.vmap(block_slots)(block_ids)
        source_index = jnp.arange(N_EXPERT, dtype=jnp.int32)[:, None, None]
        targets = ((block_ids * N_EXPERT + source_index) * CAP + slot_index).reshape(-1)
        token_index = jnp.repeat(jnp.arange(replica_rows, dtype=jnp.int32), TOPK)
        token_buf = jnp.zeros((rows_total, D), jnp.bfloat16).at[targets].set(replica_tokens[token_index])
        cot_buf = jnp.zeros((rows_total, D), jnp.bfloat16).at[targets].set(replica_cot[token_index])
        gate_buf = jnp.zeros((rows_total,), jnp.bfloat16).at[targets].set(replica_gates.reshape(-1))
        slot_grad, down_grad = lax.map(expert_work, (token_buf.reshape(EXPERTS, N_EXPERT * CAP, D), cot_buf.reshape(EXPERTS, N_EXPERT * CAP, D), gate_buf.reshape(EXPERTS, N_EXPERT * CAP), gate_weights, up_weights, down_weights))
        gate_grad = slot_grad.reshape(-1)[targets].reshape(replica_rows, TOPK)
        return (gate_grad, down_grad.reshape(N_EXPERT, HID_DEV, D))
    gate_grad, frag_grad = lax.map(replica_step, jnp.arange(N_REPLICA, dtype=jnp.int32))
    gate_grad = gate_grad.reshape(TOKENS, TOPK)
    fragment = w_down.astype(jnp.float32).reshape(N_REPLICA, N_EXPERT, HID_DEV, D)
    summed = lax.optimization_barrier(jnp.sum(fragment, axis=0))
    outer_delta = anchor - summed / N_REPLICA
    new_momentum = outer_momentum * momentum + outer_delta
    new_anchor = anchor - outer_rate * (outer_delta + outer_momentum * new_momentum)
    new_frag = (mix_weight * (fragment - inner_rate * frag_grad) + (1.0 - mix_weight) * new_anchor[None]).astype(jnp.bfloat16)
    return (gate_grad, new_frag, new_anchor, new_momentum)
```

```python
import math

import jax
import jax.numpy as jnp
from jax import lax
from jax.experimental import pallas as pl
from jax.experimental.pallas import tpu as pltpu
from jax.sharding import PartitionSpec as P

HID = 2048
OUTER_RATE = 0.7
OUTER_MOMENTUM = 0.9
MIX = 0.5
INNER_RATE = 8.0
WIN = 96
F32 = jnp.float32
BF16 = jnp.bfloat16
MESH = pl.DeviceIdType.MESH
NT = (((1,), (1,)), ((), ()))
TN = (((0,), (0,)), ((), ()))


def kernel(tok, cot, ids, gates, wg, wu, wd, anc, mom,
           out_gate, out_frag, out_anc, out_mom,
           R, T, Wg, Wu, Wd, H, ACC, GSND, GRCV, PT,
           RS, TOT, PSS, PSR, AG, ANCR, MOMR, NAS, NMS, NAR, NMR,
           GSRC, GROW, Q, QG, QR,
           y_recv, y_up, y_dn, r_recv, xp_send, xc_send, xf_send, gu_send, w_send, w_recv,
           g_send, g_recv, q_send, q_recv, rs_send, rs_recv, ag_send, ag_recv,
           am_send, am_recv, na_send, na_recv, one_send, one_recv):
    D = tok.shape[1]
    scale = 1.0 / math.sqrt(HID)
    r = lax.axis_index("replica")
    e = lax.axis_index("expert")
    c = r % 2
    z = (r // 2) % 8
    yh = r // 16
    x = e // 4
    y = e % 4
    home = (c + y) % 2 == 0
    guest = (c + y) % 2 == 1
    owner = c == yh
    mate = r + 1 - 2 * c
    peer_e = e + 1 - 2 * (e % 2)
    far = r + 16 - 32 * yh
    px = x + 1 - 2 * (x % 2)
    cx = 3 - x
    ox = 3 - px
    w0 = pl.multiple_of(32 * (x // 2), 32)
    win = pl.ds(w0, WIN)
    wot = pl.ds(pl.multiple_of(32 - 32 * (x // 2), 32), WIN)
    fill = pl.ds(pl.multiple_of(96 - 96 * (x // 2), 32), 32)
    mj = c * 8 + z
    myslot = y * 4 + x
    yu = y // 2
    yy = y + yu * (3 - 2 * y)

    def rc(src, dst, ss, rs, rep, exp):
        return pltpu.make_async_remote_copy(
            src_ref=src, dst_ref=dst, send_sem=ss, recv_sem=rs, device_id=(rep, exp), device_id_type=MESH)

    def item(i):
        p, k = i // 4, i % 4
        kk = k // 2
        f = (1 - kk) * (yy + k * (1 - 2 * yy)) + kk * k
        return p, f + yu * (3 - 2 * f)

    def member(j):
        return yh * 16 + (j % 8) * 2 + j // 8

    def loop(n, body):
        def step(i, carry):
            body(i)
            return carry
        lax.fori_loop(0, n, step, 0)

    bar = pltpu.get_barrier_semaphore()

    def hello(j):
        @pl.when(j != e)
        def _():
            pl.semaphore_signal(bar, inc=1, device_id=(r, j), device_id_type=MESH)

        @pl.when(j != mj)
        def _():
            pl.semaphore_signal(bar, inc=1, device_id=(member(j), e), device_id_type=MESH)
    loop(16, hello)
    pl.semaphore_signal(bar, inc=1, device_id=(mate, peer_e), device_id_type=MESH)
    pl.semaphore_signal(bar, inc=1, device_id=(far, e), device_id_type=MESH)

    ecol = ids[...].astype(F32)
    ebc = jnp.broadcast_to(ecol, (128, 128))
    rowi = lax.broadcasted_iota(jnp.int32, (128, 128), 0)
    lane = lax.broadcasted_iota(jnp.int32, (128, 128), 1)
    eye = (rowi == lane).astype(F32)
    lower = (lane < rowi).astype(BF16)
    ones = jnp.ones((128, 128), BF16)
    ebf = ebc.astype(BF16)
    before = jnp.dot(lower, ebf, preferred_element_type=F32)
    total1 = jnp.dot(ones, ebf, preferred_element_type=F32)
    pos = ebc * (128.0 - total1 + before) + (1.0 - ebc) * (rowi.astype(F32) - before)
    perm = (pos == lane.astype(F32)).astype(F32)
    PT[...] = perm
    permb = jnp.transpose(perm).astype(BF16)
    T[0, y] = jnp.dot(permb, tok[...], preferred_element_type=F32).astype(BF16)
    T[1, y] = jnp.dot(permb, cot[...], preferred_element_type=F32).astype(BF16)
    gp = perm * gates[...].astype(F32)
    g1 = jnp.sum(gp * ebc, axis=0, keepdims=True)
    g0 = jnp.sum(gp * (1.0 - ebc), axis=0, keepdims=True)
    GSRC[0] = g0
    GSRC[1] = g1
    RS[mj] = wd[pl.ds(pl.multiple_of(16 * mj, 16), 16), :]

    pl.semaphore_wait(bar, 32)

    def up(p, s):
        return rc(T.at[p, s], T.at[p, s], y_up.at[p, s], y_recv.at[p, s], r, e + 1)

    def down(p, s):
        return rc(T.at[p, s], T.at[p, s], y_dn.at[p, s], y_recv.at[p, s], r, e - 1)

    def line_send(p, s):
        @pl.when((s <= y) & (y < 2 + c))
        def _():
            up(p, s).start()

        @pl.when((s >= y) & (y > c))
        def _():
            down(p, s).start()

    def line_step(p, s):
        @pl.when(((s < y) & (y <= 2 + c)) | ((s > y) & (y >= c)))
        def _():
            rc(T.at[p, s], T.at[p, s], y_up.at[p, s], y_recv.at[p, s], r, e).wait_recv()
        line_send(p, s)

    line_send(0, y)

    def rs_copy(j):
        return rc(wd.at[pl.ds(pl.multiple_of(16 * j, 16), 16), :], RS.at[mj], rs_send.at[j], rs_recv.at[mj], member(j), e)

    def rs_start(j):
        @pl.when(j != mj)
        def _():
            rs_copy(j).start()
    loop(16, rs_start)

    def am_copies():
        return (rc(anc, ANCR, am_send.at[0], am_recv.at[0], mate, e),
                rc(mom, MOMR, am_send.at[1], am_recv.at[1], mate, e))

    @pl.when(c != yh)
    def _():
        for copy in am_copies():
            copy.start()

    def home_of(j):
        return (j // 2) * 4 + c + 2 * (j % 2)

    def g_copy(j):
        return rc(GSRC.at[j // 4], GROW.at[myslot], g_send.at[j], g_recv.at[myslot], r, home_of(j))

    def g_start(j):
        @pl.when(home_of(j) != e)
        def _():
            g_copy(j).start()
    loop(8, g_start)

    @pl.when(home)
    def _():
        GROW[myslot] = GSRC[x // 2]

    R[0, :, fill, :] = jnp.zeros((16, 32, D), BF16)
    R[1, :, fill, :] = jnp.zeros((16, 32, D), BF16)

    def ps_copy():
        return rc(PSS, PSR, one_send.at[0], one_recv.at[0], far, e)

    def outer_sum():
        def rs_wait(j):
            @pl.when(j != mj)
            def _():
                rc(RS.at[j], RS.at[j], rs_send.at[j], rs_recv.at[j], r, e).wait_recv()
        loop(16, rs_wait)
        TOT[...] = jnp.zeros((16, D), F32)

        def rs_add(j):
            TOT[...] += RS[j].astype(F32)
        loop(16, rs_add)

        @pl.when(c != yh)
        def _():
            PSS[...] = TOT[...].astype(BF16)
            ps_copy().start()

    def na_copies():
        return (rc(NAS, NAR, na_send.at[0], na_recv.at[0], mate, e),
                rc(NMS, NMR, na_send.at[1], na_recv.at[1], mate, e))

    def ag_copy(j):
        return rc(AG.at[mj], AG.at[mj], ag_send.at[j], ag_recv.at[mj], member(j), e)

    def agy_copy():
        return rc(AG.at[mj], AG.at[mj], one_send.at[1], ag_recv.at[mj], far, e)

    def ag_start():
        def go(j):
            @pl.when(j != mj)
            def _():
                ag_copy(j).start()
        loop(16, go)

    def nesterov(a, m, tot):
        delta = a - tot * (1.0 / 32.0)
        nm = OUTER_MOMENTUM * m + delta
        return a - OUTER_RATE * (delta + OUTER_MOMENTUM * nm), nm

    def outer_own():
        @pl.when(owner)
        def _():
            for copy in am_copies():
                copy.wait_recv()
            ps_copy().wait_recv()
            TOT[...] += PSR[...].astype(F32)
            mine = pl.ds(pl.multiple_of(8 * c, 8), 8)
            other = pl.ds(pl.multiple_of(8 - 8 * c, 8), 8)
            na, nm = nesterov(anc[...], mom[...], TOT[mine, :])
            out_anc[...] = na
            out_mom[...] = nm
            nb, nn = nesterov(ANCR[...], MOMR[...], TOT[other, :])
            NAS[...] = nb
            NMS[...] = nn
            for copy in na_copies():
                copy.start()
            TOT[mine, :] = na
            TOT[other, :] = nb
            AG[mj] = TOT[...].astype(BF16)
            agy_copy().start()
            ag_start()

    def outer_pass():
        @pl.when(c != yh)
        def _():
            agy_copy().wait_recv()
            ag_start()

    def arrived(p, slot):
        rc(R.at[p, slot, win], R.at[p, slot, win], gu_send.at[p, slot], r_recv.at[p, slot], r, e).wait_recv()

    def to_partner(p, s):
        slot = s * 4 + x
        return rc(T.at[p, s, win], R.at[p, slot, win], xp_send.at[p, s], r_recv.at[p, slot], r, px * 4 + y)

    def to_cross(p, s):
        slot = s * 4 + x
        return rc(T.at[p, s, wot], R.at[p, slot, wot], xc_send.at[p, s], r_recv.at[p, slot], r, cx * 4 + y)

    def on_to_partner(p, s):
        slot = s * 4 + cx
        return rc(R.at[p, slot, win], R.at[p, slot, win], xf_send.at[p, s], r_recv.at[p, slot], r, px * 4 + y)

    def own_copy(p, s):
        slot = s * 4 + x
        return pltpu.make_async_copy(T.at[p, s, win], R.at[p, slot, win], r_recv.at[p, slot])

    def to_guest(p, slot):
        return rc(R.at[p, slot, win], R.at[p, slot, win], gu_send.at[p, slot], r_recv.at[p, slot], mate, e)

    def own_to_guest(p, s):
        slot = s * 4 + x
        return rc(T.at[p, s, win], R.at[p, slot, win], gu_send.at[p, slot], r_recv.at[p, slot], mate, e)

    def hidden(s, wgr, wur):
        rows = R[0, pl.ds(s * 4, 4)].reshape(512, D)
        a = jnp.dot(rows, wgr[...], preferred_element_type=F32)
        u = jnp.dot(rows, wur[...], preferred_element_type=F32)
        H[s] = (a / (1.0 + jnp.exp(-a)) * u).astype(BF16)

    def grads(s, wdr):
        rows = R[1, pl.ds(s * 4, 4)].reshape(512, D)
        h = H[s].astype(F32)
        proj = lax.dot_general(rows, wdr[...], NT, preferred_element_type=F32)
        qcol = jnp.sum(h * proj, axis=1, keepdims=True)
        cols = []
        for j in range(4):
            Q[s * 4 + j] = jnp.sum(eye * qcol[j * 128:(j + 1) * 128], axis=0, keepdims=True)
            cols.append(jnp.sum(eye * GROW[s * 4 + j], axis=1, keepdims=True))
        hg = jnp.transpose((h * jnp.concatenate(cols, axis=0)).astype(BF16))
        for d in range(0, D, 256):
            ACC[:, d:d + 256] += jnp.dot(hg, rows[:, d:d + 256], preferred_element_type=F32)

    ACC[...] = jnp.zeros((256, D), F32)

    def gg_copy():
        return rc(GROW, GROW, one_send.at[2], one_recv.at[2], mate, e)

    def qg_copy():
        return rc(Q, QG, one_send.at[3], one_recv.at[3], mate, e)

    def gr_copy():
        return rc(GSND, GRCV, one_send.at[4], one_recv.at[4], mate, peer_e)

    def w_copies():
        return (rc(wg, Wg, w_send.at[0], w_recv.at[0], mate, peer_e),
                rc(wu, Wu, w_send.at[1], w_recv.at[1], mate, peer_e),
                rc(wd, Wd, w_send.at[2], w_recv.at[2], mate, peer_e))

    def q_copy(slot):
        return rc(Q.at[slot], QR.at[x * 2 + y // 2], q_send.at[slot], q_recv.at[x * 2 + y // 2],
                  r, (slot % 4) * 4 + slot // 4)

    @pl.when(home)
    def _():
        def g_wait(slot):
            @pl.when(slot != myslot)
            def _():
                rc(GROW.at[slot], GROW.at[slot], g_send.at[0], g_recv.at[slot], r, e).wait_recv()

        def step(i):
            @pl.when(i < 8)
            def _():
                p, s = item(i)
                to_partner(p, s).start()
                to_cross(p, s).start()
                own_to_guest(p, s).start()
                own_copy(p, s).start()

            @pl.when((i > 0) & (i < 9))
            def _():
                p, s = item(i - 1)
                arrived(p, s * 4 + cx)
                on_to_partner(p, s).start()
                to_guest(p, s * 4 + cx).start()
                arrived(p, s * 4 + px)
                to_guest(p, s * 4 + px).start()

            @pl.when(i == 0)
            def _():
                line_step(*item(1))
                line_send(1, y)

            @pl.when((i > 0) & (i < 7) & (i != 3))
            def _():
                line_step(*item(i + 1))

            @pl.when(i == 3)
            def _():
                loop(16, g_wait)
                gg_copy().start()

            @pl.when(i > 1)
            def _():
                p, s = item(i - 2)
                arrived(p, s * 4 + ox)
                to_guest(p, s * 4 + ox).start()
                own_copy(p, s).wait()

                @pl.when(p == 0)
                def _():
                    hidden(s, wg, wu)

                @pl.when(p == 1)
                def _():
                    grads(s, wd)

            @pl.when(i == 4)
            def _():
                outer_sum()

            @pl.when(i == 6)
            def _():
                outer_own()

            @pl.when(i == 8)
            def _():
                outer_pass()
        loop(10, step)

        qg_copy().wait_recv()
        Q[...] += QG[...]

        def q_start(slot):
            @pl.when(slot != myslot)
            def _():
                q_copy(slot).start()
        loop(16, q_start)
        QR[x * 2 + y // 2] = Q[myslot]

    @pl.when(guest)
    def _():
        ws = w_copies()
        line_send(1, y)
        for k in (1, 2, 3):
            line_step(*item(k))
        ws[0].start()
        ws[1].start()
        for k in (5, 6, 7):
            line_step(*item(k))
        ws[2].start()
        outer_sum()
        outer_own()
        outer_pass()
        ws[0].wait_recv()
        ws[1].wait_recv()

        def step(i):
            p, s = item(i)
            for col in (x, cx, px, ox):
                arrived(p, s * 4 + col)

            @pl.when(p == 0)
            def _():
                hidden(s, Wg, Wu)

            @pl.when(i == 4)
            def _():
                gg_copy().wait_recv()
                ws[2].wait_recv()

            @pl.when(p == 1)
            def _():
                grads(s, Wd)
        loop(8, step)

        GSND[...] = (scale * ACC[...]).astype(BF16)
        gr_copy().start()
        qg_copy().start()

    def q_wait(j):
        @pl.when(home_of(j) != e)
        def _():
            rc(QR.at[j], QR.at[j], q_send.at[0], q_recv.at[j], r, e).wait_recv()
    loop(8, q_wait)
    q0 = QR[0] + QR[1] + QR[2] + QR[3]
    q1 = QR[4] + QR[5] + QR[6] + QR[7]
    picked = PT[...] * (ebc * q1 + (1.0 - ebc) * q0)
    out_gate[...] = scale * jnp.sum(picked, axis=1, keepdims=True)

    def ag_wait(j):
        @pl.when(j != mj)
        def _():
            rc(AG.at[j], AG.at[j], ag_send.at[j], ag_recv.at[j], r, e).wait_recv()
    loop(16, ag_wait)

    @pl.when(c != yh)
    def _():
        for copy in na_copies():
            copy.wait_recv()
        out_anc[...] = NAR[...]
        out_mom[...] = NMR[...]

    def merge(j, grad):
        rows = pl.ds(pl.multiple_of(16 * j, 16), 16)
        out_frag[rows, :] = (MIX * wd[rows, :].astype(F32) - MIX * INNER_RATE * grad(rows)
                             + (1.0 - MIX) * AG[j].astype(F32)).astype(BF16)

    @pl.when(home)
    def _():
        loop(16, lambda j: merge(j, lambda rows: scale * ACC[rows, :]))

    @pl.when(guest)
    def _():
        gr_copy().wait_recv()
        loop(16, lambda j: merge(j, lambda rows: GRCV[rows, :].astype(F32)))

    def drain(i):
        p, s = i // 4, i % 4

        @pl.when((s <= y) & (y < 2 + c))
        def _():
            up(p, s).wait_send()

        @pl.when((s >= y) & (y > c))
        def _():
            down(p, s).wait_send()

        @pl.when(home)
        def _():
            to_partner(p, s).wait_send()
            to_cross(p, s).wait_send()
            on_to_partner(p, s).wait_send()
            for col in range(4):
                to_guest(p, s * 4 + col).wait_send()
    loop(8, drain)

    def drain_small(j):
        @pl.when(j != mj)
        def _():
            rs_copy(j).wait_send()
            ag_copy(j).wait_send()

        @pl.when(home & (j != myslot))
        def _():
            q_copy(j).wait_send()
    loop(16, drain_small)

    def drain_g(j):
        @pl.when(home_of(j) != e)
        def _():
            g_copy(j).wait_send()
    loop(8, drain_g)

    @pl.when(home)
    def _():
        gg_copy().wait_send()

    @pl.when(guest)
    def _():
        for copy in w_copies():
            copy.wait_send()
        gr_copy().wait_send()
        qg_copy().wait_send()

    @pl.when(owner)
    def _():
        agy_copy().wait_send()
        for copy in na_copies():
            copy.wait_send()

    @pl.when(c != yh)
    def _():
        ps_copy().wait_send()
        for copy in am_copies():
            copy.wait_send()


def per_device(tokens, cotangent, expert_ids, gate_values, w_gate, w_up, w_down, anchor, momentum):
    D = tokens.shape[1]
    vm = pl.BlockSpec(memory_space=pltpu.VMEM)
    dma = pltpu.SemaphoreType.DMA
    V = pltpu.VMEM
    gate, frag, anc, mom = pl.pallas_call(
        kernel,
        out_shape=(
            jax.ShapeDtypeStruct((128, 1), F32),
            jax.ShapeDtypeStruct((256, D), BF16),
            jax.ShapeDtypeStruct((8, D), F32),
            jax.ShapeDtypeStruct((8, D), F32),
        ),
        in_specs=[vm] * 9,
        out_specs=[vm] * 4,
        scratch_shapes=[
            V((2, 16, 128, D), BF16), V((2, 4, 128, D), BF16),
            V((D, 256), BF16), V((D, 256), BF16), V((256, D), BF16),
            V((4, 512, 256), BF16), V((256, D), F32), V((256, D), BF16), V((256, D), BF16), V((128, 128), F32),
            V((16, 16, D), BF16), V((16, D), F32), V((16, D), BF16), V((16, D), BF16), V((16, 16, D), BF16),
            V((8, D), F32), V((8, D), F32), V((8, D), F32), V((8, D), F32), V((8, D), F32), V((8, D), F32),
            V((2, 1, 128), F32), V((16, 1, 128), F32), V((16, 1, 128), F32), V((16, 1, 128), F32), V((8, 1, 128), F32),
            dma((2, 4)), dma((2, 4)), dma((2, 4)), dma((2, 16)), dma((2, 4)), dma((2, 4)), dma((2, 4)), dma((2, 16)),
            dma((3,)), dma((3,)),
            dma((8,)), dma((16,)), dma((16,)), dma((8,)), dma((16,)), dma((16,)), dma((16,)), dma((16,)),
            dma((2,)), dma((2,)), dma((2,)), dma((2,)), dma((5,)), dma((5,)),
        ],
        compiler_params=pltpu.CompilerParams(
            collective_id=0, has_side_effects=True, vmem_limit_bytes=58 * 1024 * 1024),
        name="step",
    )(tokens, cotangent, expert_ids, gate_values, w_gate[0], w_up[0], w_down[0], anchor[0], momentum[0])
    return gate, frag[None, None], anc[None], mom[None]


def solution(mesh):
    return jax.shard_map(
        per_device,
        mesh=mesh,
        in_specs=(
            P(("replica", "expert"), None),
            P(("replica", "expert"), None),
            P(("replica", "expert"), None),
            P(("replica", "expert"), None),
            P("replica", None, "expert"),
            P("replica", None, "expert"),
            P("replica", "expert", None),
            P("expert", "replica", None),
            P("expert", "replica", None),
        ),
        out_specs=(
            P(("replica", "expert"), None),
            P("replica", "expert", None, None),
            P("expert", "replica", None),
            P("expert", "replica", None),
        ),
        check_vma=False,
    )
```

```python
import math

import jax
import jax.numpy as jnp
from jax import lax
from jax.experimental import pallas as pl
from jax.experimental.pallas import tpu as pltpu
from jax.sharding import PartitionSpec as P

HID = 2048
OUTER_RATE = 0.7
OUTER_MOMENTUM = 0.9
MIX = 0.5
INNER_RATE = 8.0
WIN = 96
F32 = jnp.float32
BF16 = jnp.bfloat16
MESH = pl.DeviceIdType.MESH
NT = (((1,), (1,)), ((), ()))
TN = (((0,), (0,)), ((), ()))


def kernel(tok, cot, ids, gates, wg, wu, wd, anc, mom,
           out_gate, out_frag, out_anc, out_mom,
           R, T, Wg, Wu, Wd, Wo, H, ACC, GSND, GRCV, PT,
           RS, TOT, PSS, PSR, AG, ANCR, MOMR, NAS, NMS, NAR, NMR,
           GSRC, GROW, Q, QG, QR,
           y_recv, y_up, y_dn, r_recv, xp_send, xc_send, xf_send, gu_send, w_send, w_recv,
           g_send, g_recv, q_send, q_recv, rs_send, rs_recv, ag_send, ag_recv,
           am_send, am_recv, na_send, na_recv, one_send, one_recv, l_sem):
    D = tok.shape[1]
    scale = 1.0 / math.sqrt(HID)
    r = lax.axis_index("replica")
    e = lax.axis_index("expert")
    c = r % 2
    z = (r // 2) % 8
    yh = r // 16
    x = e // 4
    y = e % 4
    home = (c + y) % 2 == 0
    guest = (c + y) % 2 == 1
    owner = c == yh
    mate = r + 1 - 2 * c
    peer_e = e + 1 - 2 * (e % 2)
    far = r + 16 - 32 * yh
    px = x + 1 - 2 * (x % 2)
    cx = 3 - x
    ox = 3 - px
    w0 = pl.multiple_of(32 * (x // 2), 32)
    win = pl.ds(w0, WIN)
    wot = pl.ds(pl.multiple_of(32 - 32 * (x // 2), 32), WIN)
    fill = pl.ds(pl.multiple_of(96 - 96 * (x // 2), 32), 32)
    mj = c * 8 + z
    myslot = y * 4 + x
    yu = y // 2
    yy = y + yu * (3 - 2 * y)

    def rc(src, dst, ss, rs, rep, exp):
        return pltpu.make_async_remote_copy(
            src_ref=src, dst_ref=dst, send_sem=ss, recv_sem=rs, device_id=(rep, exp), device_id_type=MESH)

    def item(i):
        p, k = i % 2, i // 2
        kk = k // 2
        f = (1 - kk) * (yy + k * (1 - 2 * yy)) + kk * k
        return p, f + yu * (3 - 2 * f)

    def member(j):
        return yh * 16 + (j % 8) * 2 + j // 8

    def loop(n, body):
        def step(i, carry):
            body(i)
            return carry
        lax.fori_loop(0, n, step, 0)

    own = pltpu.make_async_copy(wd, Wo, l_sem.at[0])
    own.start()

    def w_local():
        return [pltpu.make_async_copy(a, b, l_sem.at[n + 1]) for n, (a, b) in enumerate(((wg, Wg), (wu, Wu), (wd, Wd)))]

    @pl.when(home)
    def _():
        for copy in w_local():
            copy.start()

    bar = pltpu.get_barrier_semaphore()

    def hello(j):
        @pl.when(j != e)
        def _():
            pl.semaphore_signal(bar, inc=1, device_id=(r, j), device_id_type=MESH)

        @pl.when(j != mj)
        def _():
            pl.semaphore_signal(bar, inc=1, device_id=(member(j), e), device_id_type=MESH)
    loop(16, hello)
    pl.semaphore_signal(bar, inc=1, device_id=(mate, peer_e), device_id_type=MESH)
    pl.semaphore_signal(bar, inc=1, device_id=(far, e), device_id_type=MESH)

    rowi = lax.broadcasted_iota(jnp.int32, (128, 128), 0)
    lane = lax.broadcasted_iota(jnp.int32, (128, 128), 1)
    eye = (rowi == lane).astype(F32)
    ecol = jnp.sum(eye * ids[...].astype(F32), axis=1, keepdims=True)
    gcol = jnp.sum(eye * gates[...].astype(F32), axis=1, keepdims=True)
    ebc = jnp.broadcast_to(ecol, (128, 128))
    lower = (lane < rowi).astype(BF16)
    ones = jnp.ones((128, 128), BF16)
    ebf = ebc.astype(BF16)
    before = jnp.dot(lower, ebf, preferred_element_type=F32)
    total1 = jnp.dot(ones, ebf, preferred_element_type=F32)
    pos = ebc * (128.0 - total1 + before) + (1.0 - ebc) * (rowi.astype(F32) - before)
    perm = (pos == lane.astype(F32)).astype(F32)
    PT[...] = perm
    permb = jnp.transpose(perm).astype(BF16)
    T[0, y] = jnp.dot(permb, tok[...], preferred_element_type=F32).astype(BF16)
    T[1, y] = jnp.dot(permb, cot[...], preferred_element_type=F32).astype(BF16)
    gp = perm * gcol
    g1 = jnp.sum(gp * ebc, axis=0, keepdims=True)
    g0 = jnp.sum(gp * (1.0 - ebc), axis=0, keepdims=True)
    GSRC[0] = g0
    GSRC[1] = g1
    mine16 = pltpu.make_async_copy(wd.at[pl.ds(pl.multiple_of(16 * mj, 16), 16), :], RS.at[mj], l_sem.at[4])
    mine16.start()

    pl.semaphore_wait(bar, 32)

    def up(p, s):
        return rc(T.at[p, s], T.at[p, s], y_up.at[p, s], y_recv.at[p, s], r, e + 1)

    def down(p, s):
        return rc(T.at[p, s], T.at[p, s], y_dn.at[p, s], y_recv.at[p, s], r, e - 1)

    def line_send(p, s):
        @pl.when((s <= y) & (y < 2 + c))
        def _():
            up(p, s).start()

        @pl.when((s >= y) & (y > c))
        def _():
            down(p, s).start()

    def line_drain(p, s):
        @pl.when((s <= y) & (y < 2 + c))
        def _():
            up(p, s).wait_send()

        @pl.when((s >= y) & (y > c))
        def _():
            down(p, s).wait_send()

    def line_step(p, s):
        @pl.when(((s < y) & (y <= 2 + c)) | ((s > y) & (y >= c)))
        def _():
            rc(T.at[p, s], T.at[p, s], y_up.at[p, s], y_recv.at[p, s], r, e).wait_recv()
        line_send(p, s)

    line_send(0, y)
    line_send(1, y)

    def rs_copy(j):
        return rc(wd.at[pl.ds(pl.multiple_of(16 * j, 16), 16), :], RS.at[mj], rs_send.at[j], rs_recv.at[mj], member(j), e)

    def rs_start(j):
        @pl.when(j != mj)
        def _():
            rs_copy(j).start()
    loop(16, rs_start)

    def am_copies():
        return (rc(anc, ANCR, am_send.at[0], am_recv.at[0], mate, e),
                rc(mom, MOMR, am_send.at[1], am_recv.at[1], mate, e))

    @pl.when(c != yh)
    def _():
        for copy in am_copies():
            copy.start()

    def home_of(j):
        return (j // 2) * 4 + c + 2 * (j % 2)

    def g_copy(j):
        return rc(GSRC.at[j // 4], GROW.at[myslot], g_send.at[j], g_recv.at[myslot], r, home_of(j))

    def g_start(j):
        @pl.when(home_of(j) != e)
        def _():
            g_copy(j).start()
    loop(8, g_start)

    @pl.when(home)
    def _():
        GROW[myslot] = GSRC[x // 2]

    R[0, :, fill, :] = jnp.zeros((16, 32, D), BF16)
    R[1, :, fill, :] = jnp.zeros((16, 32, D), BF16)

    def ps_copy():
        return rc(PSS, PSR, one_send.at[0], one_recv.at[0], far, e)

    def outer_sum():
        def rs_wait(j):
            @pl.when(j != mj)
            def _():
                rc(RS.at[j], RS.at[j], rs_send.at[j], rs_recv.at[j], r, e).wait_recv()
        loop(16, rs_wait)
        pltpu.make_async_copy(wd.at[pl.ds(pl.multiple_of(16 * mj, 16), 16), :], RS.at[mj], l_sem.at[4]).wait()
        TOT[...] = jnp.zeros((16, D), F32)

        def rs_add(j):
            TOT[...] += RS[j].astype(F32)
        loop(16, rs_add)

        @pl.when(c != yh)
        def _():
            PSS[...] = TOT[...].astype(BF16)
            ps_copy().start()

    def na_copies():
        return (rc(NAS, NAR, na_send.at[0], na_recv.at[0], mate, e),
                rc(NMS, NMR, na_send.at[1], na_recv.at[1], mate, e))

    def ag_copy(j):
        return rc(AG.at[mj], AG.at[mj], ag_send.at[j], ag_recv.at[mj], member(j), e)

    def agy_copy():
        return rc(AG.at[mj], AG.at[mj], one_send.at[1], ag_recv.at[mj], far, e)

    def ag_start():
        def go(j):
            @pl.when(j != mj)
            def _():
                ag_copy(j).start()
        loop(16, go)

    def nesterov(a, m, tot):
        delta = a - tot * (1.0 / 32.0)
        nm = OUTER_MOMENTUM * m + delta
        return a - OUTER_RATE * (delta + OUTER_MOMENTUM * nm), nm

    def outer_own():
        @pl.when(owner)
        def _():
            for copy in am_copies():
                copy.wait_recv()
            ps_copy().wait_recv()
            TOT[...] += PSR[...].astype(F32)
            mine = pl.ds(pl.multiple_of(8 * c, 8), 8)
            other = pl.ds(pl.multiple_of(8 - 8 * c, 8), 8)
            na, nm = nesterov(anc[...], mom[...], TOT[mine, :])
            out_anc[...] = na
            out_mom[...] = nm
            nb, nn = nesterov(ANCR[...], MOMR[...], TOT[other, :])
            NAS[...] = nb
            NMS[...] = nn
            for copy in na_copies():
                copy.start()
            TOT[mine, :] = na
            TOT[other, :] = nb
            AG[mj] = TOT[...].astype(BF16)
            agy_copy().start()
            ag_start()

    def outer_pass():
        @pl.when(c != yh)
        def _():
            agy_copy().wait_recv()
            ag_start()

    def arrived(p, slot):
        rc(R.at[p, slot, win], R.at[p, slot, win], gu_send.at[p, slot], r_recv.at[p, slot], r, e).wait_recv()

    def to_partner(p, s):
        slot = s * 4 + x
        return rc(T.at[p, s, win], R.at[p, slot, win], xp_send.at[p, s], r_recv.at[p, slot], r, px * 4 + y)

    def to_cross(p, s):
        slot = s * 4 + x
        return rc(T.at[p, s, wot], R.at[p, slot, wot], xc_send.at[p, s], r_recv.at[p, slot], r, cx * 4 + y)

    def on_to_partner(p, s):
        slot = s * 4 + cx
        return rc(R.at[p, slot, win], R.at[p, slot, win], xf_send.at[p, s], r_recv.at[p, slot], r, px * 4 + y)

    def own_copy(p, s):
        slot = s * 4 + x
        return pltpu.make_async_copy(T.at[p, s, win], R.at[p, slot, win], r_recv.at[p, slot])

    def to_guest(p, slot):
        return rc(R.at[p, slot, win], R.at[p, slot, win], gu_send.at[p, slot], r_recv.at[p, slot], mate, e)

    def own_to_guest(p, s):
        slot = s * 4 + x
        return rc(T.at[p, s, win], R.at[p, slot, win], gu_send.at[p, slot], r_recv.at[p, slot], mate, e)

    def hidden(s):
        rows = R[0, pl.ds(s * 4, 4)].reshape(512, D)
        a = jnp.dot(rows, Wg[...], preferred_element_type=F32)
        u = jnp.dot(rows, Wu[...], preferred_element_type=F32)
        H[s] = (a / (1.0 + jnp.exp(-a)) * u).astype(BF16)

    def grads(s):
        rows = R[1, pl.ds(s * 4, 4)].reshape(512, D)
        cols = [jnp.sum(eye * GROW[s * 4 + j], axis=1, keepdims=True) for j in range(4)]
        hg = jnp.transpose((H[s].astype(F32) * jnp.concatenate(cols, axis=0)).astype(BF16))
        for d in range(0, D, 256):
            ACC[:, d:d + 256] += jnp.dot(hg, rows[:, d:d + 256], preferred_element_type=F32)

    def router(s):
        rows = R[1, pl.ds(s * 4, 4)].reshape(512, D)
        proj = lax.dot_general(rows, Wd[...], NT, preferred_element_type=F32)
        qcol = jnp.sum(H[s].astype(F32) * proj, axis=1, keepdims=True)
        for j in range(4):
            Q[s * 4 + j] = jnp.sum(eye * qcol[j * 128:(j + 1) * 128], axis=0, keepdims=True)

    ACC[...] = jnp.zeros((256, D), F32)

    def gg_copy():
        return rc(GROW, GROW, one_send.at[2], one_recv.at[2], mate, e)

    def qg_copy():
        return rc(Q, QG, one_send.at[3], one_recv.at[3], mate, e)

    def gr_copy():
        return rc(GSND, GRCV, one_send.at[4], one_recv.at[4], mate, peer_e)

    def w_copies():
        return (rc(wg, Wg, w_send.at[0], w_recv.at[0], mate, peer_e),
                rc(wu, Wu, w_send.at[1], w_recv.at[1], mate, peer_e),
                rc(wd, Wd, w_send.at[2], w_recv.at[2], mate, peer_e))

    def q_copy(slot):
        return rc(Q.at[slot], QR.at[x * 2 + y // 2], q_send.at[slot], q_recv.at[x * 2 + y // 2],
                  r, (slot % 4) * 4 + slot // 4)

    @pl.when(home)
    def _():
        def g_wait(slot):
            @pl.when(slot != myslot)
            def _():
                rc(GROW.at[slot], GROW.at[slot], g_send.at[0], g_recv.at[slot], r, e).wait_recv()

        def step(i):
            @pl.when(i < 8)
            def _():
                p, s = item(i)
                to_partner(p, s).start()
                to_cross(p, s).start()
                own_to_guest(p, s).start()
                own_copy(p, s).start()

            @pl.when((i > 0) & (i < 9))
            def _():
                p, s = item(i - 1)
                arrived(p, s * 4 + cx)
                on_to_partner(p, s).start()
                to_guest(p, s * 4 + cx).start()
                arrived(p, s * 4 + px)
                to_guest(p, s * 4 + px).start()

            @pl.when((i > 0) & (i < 7))
            def _():
                line_step(*item(i + 1))

            @pl.when(i == 2)
            def _():
                loop(16, g_wait)
                gg_copy().start()
                for copy in w_local():
                    copy.wait()

            @pl.when(i > 1)
            def _():
                p, s = item(i - 2)
                arrived(p, s * 4 + ox)
                to_guest(p, s * 4 + ox).start()
                own_copy(p, s).wait()

                @pl.when(p == 0)
                def _():
                    hidden(s)

                @pl.when(p == 1)
                def _():
                    grads(s)
                    router(s)

            @pl.when(i == 4)
            def _():
                outer_sum()

            @pl.when(i == 6)
            def _():
                outer_own()

            @pl.when(i == 8)
            def _():
                outer_pass()
        loop(10, step)

        qg_copy().wait_recv()
        Q[...] += QG[...]

        def q_start(slot):
            @pl.when(slot != myslot)
            def _():
                q_copy(slot).start()
        loop(16, q_start)
        QR[x * 2 + y // 2] = Q[myslot]

    @pl.when(guest)
    def _():
        ws = w_copies()

        @pl.when((y == 0) | (y == 3))
        def _():
            for p in (0, 1):
                line_drain(p, y)
            ws[0].start()
            outer_sum()
            ws[0].wait_send()
            ws[1].start()
            outer_own()
            ws[1].wait_send()
            ws[2].start()
            outer_pass()

        @pl.when((y == 1) | (y == 2))
        def _():
            ws[0].start()
            for i in (2, 3, 4, 5):
                line_step(*item(i))
            ws[0].wait_send()
            ws[1].start()
            outer_sum()
            for i in (6, 7):
                line_step(*item(i))
            ws[1].wait_send()
            ws[2].start()
            outer_own()
            outer_pass()
        ws[0].wait_recv()
        ws[1].wait_recv()
        gg_copy().wait_recv()

        def step(k):
            s = item(2 * k)[1]
            for col in (x, cx, px, ox):
                arrived(0, s * 4 + col)
            hidden(s)
            for col in (x, cx, px, ox):
                arrived(1, s * 4 + col)
            grads(s)
        loop(4, step)

        GSND[...] = (scale * ACC[...]).astype(BF16)
        gr_copy().start()
        ws[2].wait_recv()
        loop(4, router)
        qg_copy().start()

    def q_wait(j):
        @pl.when(home_of(j) != e)
        def _():
            rc(QR.at[j], QR.at[j], q_send.at[0], q_recv.at[j], r, e).wait_recv()
    loop(8, q_wait)
    q0 = QR[0] + QR[1] + QR[2] + QR[3]
    q1 = QR[4] + QR[5] + QR[6] + QR[7]
    picked = PT[...] * (ebc * q1 + (1.0 - ebc) * q0)
    out_gate[...] = scale * jnp.sum(eye * jnp.sum(picked, axis=1, keepdims=True), axis=0, keepdims=True)

    def ag_wait(j):
        @pl.when(j != mj)
        def _():
            rc(AG.at[j], AG.at[j], ag_send.at[j], ag_recv.at[j], r, e).wait_recv()
    loop(16, ag_wait)

    @pl.when(c != yh)
    def _():
        for copy in na_copies():
            copy.wait_recv()
        out_anc[...] = NAR[...]
        out_mom[...] = NMR[...]

    own.wait()

    def merge(j, grad):
        rows = pl.ds(pl.multiple_of(16 * j, 16), 16)
        out_frag[rows, :] = (MIX * Wo[rows, :].astype(F32) - MIX * INNER_RATE * grad(rows)
                             + (1.0 - MIX) * AG[j].astype(F32)).astype(BF16)

    @pl.when(home)
    def _():
        loop(16, lambda j: merge(j, lambda rows: scale * ACC[rows, :]))

    @pl.when(guest)
    def _():
        gr_copy().wait_recv()
        loop(16, lambda j: merge(j, lambda rows: GRCV[rows, :].astype(F32)))

    def drain(i):
        p, s = i // 4, i % 4

        @pl.when(home | (y == 1) | (y == 2))
        def _():
            line_drain(p, s)

        @pl.when(home)
        def _():
            to_partner(p, s).wait_send()
            to_cross(p, s).wait_send()
            on_to_partner(p, s).wait_send()
            for col in range(4):
                to_guest(p, s * 4 + col).wait_send()
    loop(8, drain)

    def drain_small(j):
        @pl.when(j != mj)
        def _():
            rs_copy(j).wait_send()
            ag_copy(j).wait_send()

        @pl.when(home & (j != myslot))
        def _():
            q_copy(j).wait_send()
    loop(16, drain_small)

    def drain_g(j):
        @pl.when(home_of(j) != e)
        def _():
            g_copy(j).wait_send()
    loop(8, drain_g)

    @pl.when(home)
    def _():
        gg_copy().wait_send()

    @pl.when(guest)
    def _():
        w_copies()[2].wait_send()
        gr_copy().wait_send()
        qg_copy().wait_send()

    @pl.when(owner)
    def _():
        agy_copy().wait_send()
        for copy in na_copies():
            copy.wait_send()

    @pl.when(c != yh)
    def _():
        ps_copy().wait_send()
        for copy in am_copies():
            copy.wait_send()


def handover(a, b, c, d, a2, b2, c2, d2):
    a2[...] = a[...]
    b2[...] = b[...]
    c2[...] = c[...]
    d2[...] = d[...]


def per_device(tokens, cotangent, expert_ids, gate_values, w_gate, w_up, w_down, anchor, momentum):
    D = tokens.shape[1]
    vm = pl.BlockSpec(memory_space=pltpu.VMEM)
    dma = pltpu.SemaphoreType.DMA
    V = pltpu.VMEM
    gate, frag, anc, mom = pl.pallas_call(
        kernel,
        out_shape=(
            jax.ShapeDtypeStruct((1, 128), F32),
            jax.ShapeDtypeStruct((256, D), BF16),
            jax.ShapeDtypeStruct((8, D), F32),
            jax.ShapeDtypeStruct((8, D), F32),
        ),
        in_specs=[vm] * 4 + [pl.BlockSpec(memory_space=pl.ANY)] * 3 + [vm] * 2,
        out_specs=[vm] * 4,
        scratch_shapes=[
            V((2, 16, 128, D), BF16), V((2, 4, 128, D), BF16),
            V((D, 256), BF16), V((D, 256), BF16), V((256, D), BF16), V((256, D), BF16),
            V((4, 512, 256), BF16), V((256, D), F32), V((256, D), BF16), V((256, D), BF16), V((128, 128), F32),
            V((16, 16, D), BF16), V((16, D), F32), V((16, D), BF16), V((16, D), BF16), V((16, 16, D), BF16),
            V((8, D), F32), V((8, D), F32), V((8, D), F32), V((8, D), F32), V((8, D), F32), V((8, D), F32),
            V((2, 1, 128), F32), V((16, 1, 128), F32), V((16, 1, 128), F32), V((16, 1, 128), F32), V((8, 1, 128), F32),
            dma((2, 4)), dma((2, 4)), dma((2, 4)), dma((2, 16)), dma((2, 4)), dma((2, 4)), dma((2, 4)), dma((2, 16)),
            dma((3,)), dma((3,)),
            dma((8,)), dma((16,)), dma((16,)), dma((8,)), dma((16,)), dma((16,)), dma((16,)), dma((16,)),
            dma((2,)), dma((2,)), dma((2,)), dma((2,)), dma((5,)), dma((5,)), dma((5,)),
        ],
        compiler_params=pltpu.CompilerParams(
            collective_id=0, has_side_effects=True, vmem_limit_bytes=58 * 1024 * 1024),
        name="step",
    )(tokens, cotangent, expert_ids.reshape(1, 128), gate_values.reshape(1, 128), w_gate[0], w_up[0], w_down[0], anchor[0], momentum[0])
    gate, frag, anc, mom = pl.pallas_call(
        handover,
        out_shape=(
            jax.ShapeDtypeStruct((1, 128), F32),
            jax.ShapeDtypeStruct((256, D), BF16),
            jax.ShapeDtypeStruct((8, D), F32),
            jax.ShapeDtypeStruct((8, D), F32),
        ),
        in_specs=[vm] * 4,
        out_specs=[vm] * 4,
        compiler_params=pltpu.CompilerParams(vmem_limit_bytes=58 * 1024 * 1024),
        name="handover",
    )(gate, frag, anc, mom)
    return gate.reshape(128, 1), frag[None, None], anc[None], mom[None]


def solution(mesh):
    return jax.shard_map(
        per_device,
        mesh=mesh,
        in_specs=(
            P(("replica", "expert"), None),
            P(("replica", "expert"), None),
            P(("replica", "expert"), None),
            P(("replica", "expert"), None),
            P("replica", None, "expert"),
            P("replica", None, "expert"),
            P("replica", "expert", None),
            P("expert", "replica", None),
            P("expert", "replica", None),
        ),
        out_specs=(
            P(("replica", "expert"), None),
            P("replica", "expert", None, None),
            P("expert", "replica", None),
            P("expert", "replica", None),
        ),
        check_vma=False,
    )
```

```python
import math

import jax
import jax.numpy as jnp
from jax import lax
from jax.experimental import pallas as pl
from jax.experimental.pallas import tpu as pltpu
from jax.sharding import PartitionSpec as P

HID = 2048
OUTER_RATE = 0.7
OUTER_MOMENTUM = 0.9
MIX = 0.5
INNER_RATE = 8.0
WIN = 96
F32 = jnp.float32
BF16 = jnp.bfloat16
MESH = pl.DeviceIdType.MESH
NT = (((1,), (1,)), ((), ()))
TN = (((0,), (0,)), ((), ()))


def kernel(tok, cot, ids, gates, wg, wu, wd, anc, mom,
           out_gate, out_frag, out_anc, out_mom,
           R, T, WU, WD, Wo, H, ACC, GSND, GRCV, PT,
           CH, RSS, RS, TOT, PSS, PSR, AG, ANCR, MOMR, NAS, NMS, NAR, NMR,
           GSRC, GROW, Q, QG, QR,
           y_recv, y_up, y_dn, r_recv, xp_send, xc_send, xf_send, gu_send, w_send, w_recv,
           g_send, g_recv, q_send, q_recv, rs_send, rs_recv, ag_send, ag_recv,
           am_send, am_recv, na_send, na_recv, one_send, one_recv, l_sem, gr_send, gr_recv):
    D = tok.shape[1]
    HALF = D // 2
    scale = 1.0 / math.sqrt(HID)
    r = lax.axis_index("replica")
    e = lax.axis_index("expert")
    c = r % 2
    z = (r // 2) % 8
    yh = r // 16
    x = e // 4
    y = e % 4
    home = (c + y) % 2 == 0
    guest = (c + y) % 2 == 1
    owner = c == yh
    mid = (y == 1) | (y == 2)
    edge = (y == 0) | (y == 3)
    other_e = e - 2 * y + 3
    mate = r + 1 - 2 * c
    peer_e = e + 1 - 2 * (e % 2)
    far = r + 16 - 32 * yh
    px = x + 1 - 2 * (x % 2)
    cx = 3 - x
    ox = 3 - px
    w0 = pl.multiple_of(32 * (x // 2), 32)
    win = pl.ds(w0, WIN)
    wot = pl.ds(pl.multiple_of(32 - 32 * (x // 2), 32), WIN)
    fill = pl.ds(pl.multiple_of(96 - 96 * (x // 2), 32), 32)
    mj = c * 8 + z
    myslot = y * 4 + x
    yu = y // 2
    yy = y + yu * (3 - 2 * y)

    def rc(src, dst, ss, rs, rep, exp):
        return pltpu.make_async_remote_copy(
            src_ref=src, dst_ref=dst, send_sem=ss, recv_sem=rs, device_id=(rep, exp), device_id_type=MESH)

    def item(i):
        ge4, ge13 = (i + 12) // 16, (i + 3) // 16
        k = ge4 * (1 - ge13) * ((i + 11) // 3 - 4) + ge13 * (i - 12)
        p = (1 - ge4) * i + ge4 * (1 - ge13) * ((i + 11) % 3) + ge13 * 3
        kk = k // 2
        f = (1 - kk) * (yy + k * (1 - 2 * yy)) + kk * k
        return p, f + yu * (3 - 2 * f)

    def member(j):
        return yh * 16 + j * 2 + c

    def loop(n, body):
        def step(i, carry):
            body(i)
            return carry
        lax.fori_loop(0, n, step, 0)

    own = pltpu.make_async_copy(wd, Wo, l_sem.at[0])
    own.start()

    def w_local():
        pairs = []
        for n in (0, 1):
            cols = pl.ds(128 * n, 128)
            pairs += [(wg.at[:, cols], WU.at[n, :, pl.ds(0, 128)]), (wu.at[:, cols], WU.at[n, :, pl.ds(128, 128)]),
                      (wd.at[cols, :], WD.at[n])]
        return [pltpu.make_async_copy(a, b, l_sem.at[2 + n]) for n, (a, b) in enumerate(pairs)]

    @pl.when(home)
    def _():
        for copy in w_local():
            copy.start()

    bar = pltpu.get_barrier_semaphore()

    def hello(j):
        @pl.when(j != e)
        def _():
            pl.semaphore_signal(bar, inc=1, device_id=(r, j), device_id_type=MESH)

    loop(16, hello)

    def hello_z(j):
        @pl.when(j != z)
        def _():
            pl.semaphore_signal(bar, inc=1, device_id=(member(j), e), device_id_type=MESH)
    loop(8, hello_z)
    pl.semaphore_signal(bar, inc=1, device_id=(mate, e), device_id_type=MESH)
    pl.semaphore_signal(bar, inc=1, device_id=(mate, peer_e), device_id_type=MESH)
    pl.semaphore_signal(bar, inc=1, device_id=(far, e), device_id_type=MESH)

    @pl.when(mid)
    def _():
        pl.semaphore_signal(bar, inc=1, device_id=(mate, other_e), device_id_type=MESH)

    rowi = lax.broadcasted_iota(jnp.int32, (128, 128), 0)
    lane = lax.broadcasted_iota(jnp.int32, (128, 128), 1)
    eye = (rowi == lane).astype(F32)
    ecol = jnp.sum(eye * ids[...].astype(F32), axis=1, keepdims=True)
    gcol = jnp.sum(eye * gates[...].astype(F32), axis=1, keepdims=True)
    ebc = jnp.broadcast_to(ecol, (128, 128))
    lower = (lane < rowi).astype(BF16)
    ones = jnp.ones((128, 128), BF16)
    ebf = ebc.astype(BF16)
    before = jnp.dot(lower, ebf, preferred_element_type=F32)
    total1 = jnp.dot(ones, ebf, preferred_element_type=F32)
    pos = ebc * (128.0 - total1 + before) + (1.0 - ebc) * (rowi.astype(F32) - before)
    perm = (pos == lane.astype(F32)).astype(F32)
    PT[...] = perm
    permb = jnp.transpose(perm).astype(BF16)
    for p, rows in enumerate((tok, tok, cot, cot)):
        cols = pl.ds(HALF * (p % 2), HALF)
        T[p, y] = jnp.dot(permb, rows[:, cols], preferred_element_type=F32).astype(BF16)
    gp = perm * gcol
    g1 = jnp.sum(gp * ebc, axis=0, keepdims=True)
    g0 = jnp.sum(gp * (1.0 - ebc), axis=0, keepdims=True)
    GSRC[0] = g0
    GSRC[1] = g1

    pl.semaphore_wait(bar, 25 + y * (3 - y) // 2)

    def up(p, s):
        return rc(T.at[p, s], T.at[p, s], y_up.at[p, s], y_recv.at[p, s], r, e + 1)

    def down(p, s):
        return rc(T.at[p, s], T.at[p, s], y_dn.at[p, s], y_recv.at[p, s], r, e - 1)

    def line_send(p, s):
        @pl.when((s <= y) & (y < 2 + c))
        def _():
            up(p, s).start()

        @pl.when((s >= y) & (y > c))
        def _():
            down(p, s).start()

    def line_drain(p, s):
        @pl.when((s <= y) & (y < 2 + c))
        def _():
            up(p, s).wait_send()

        @pl.when((s >= y) & (y > c))
        def _():
            down(p, s).wait_send()

    def line_step(p, s):
        @pl.when(((s < y) & (y <= 2 + c)) | ((s > y) & (y >= c)))
        def _():
            rc(T.at[p, s], T.at[p, s], y_up.at[p, s], y_recv.at[p, s], r, e).wait_recv()
        line_send(p, s)

    line_send(0, y)
    line_send(1, y)

    def ch_copy():
        return rc(wd.at[pl.ds(pl.multiple_of(128 - 128 * c, 128), 128), :], CH, one_send.at[4], one_recv.at[4], mate, e)

    def rs_copy(j):
        return rc(RSS.at[j], RS.at[z], rs_send.at[j], rs_recv.at[z], member(j), e)

    def outer_start():
        own.wait()
        ch_copy().wait_recv()

        def pair(j):
            rows = pl.ds(pl.multiple_of(16 * j, 16), 16)
            mine = Wo[pl.ds(pl.multiple_of(128 * c + 16 * j, 16), 16), :]
            RSS[j] = (mine.astype(F32) + CH[rows, :].astype(F32)).astype(BF16)
        loop(8, pair)
        RS[z] = RSS[z]

        def rs_start(j):
            @pl.when(j != z)
            def _():
                rs_copy(j).start()
        loop(8, rs_start)

    def am_copies():
        return (rc(anc, ANCR, am_send.at[0], am_recv.at[0], mate, e),
                rc(mom, MOMR, am_send.at[1], am_recv.at[1], mate, e))

    def home_of(j):
        return (j // 2) * 4 + c + 2 * (j % 2)

    def g_copy(j):
        return rc(GSRC.at[j // 4], GROW.at[myslot], g_send.at[j], g_recv.at[myslot], r, home_of(j))

    def g_start(j):
        @pl.when(home_of(j) != e)
        def _():
            g_copy(j).start()
    def ps_copy():
        return rc(PSS, PSR, one_send.at[0], one_recv.at[0], far, e)

    def outer_sum():
        def rs_wait(j):
            @pl.when(j != z)
            def _():
                rc(RS.at[j], RS.at[j], rs_send.at[j], rs_recv.at[j], r, e).wait_recv()
        loop(8, rs_wait)
        TOT[...] = jnp.zeros((16, D), F32)

        def rs_add(j):
            TOT[...] += RS[j].astype(F32)
        loop(8, rs_add)

        @pl.when(c != yh)
        def _():
            PSS[...] = TOT[...].astype(BF16)
            ps_copy().start()

    def na_copies():
        return (rc(NAS, NAR, na_send.at[0], na_recv.at[0], mate, e),
                rc(NMS, NMR, na_send.at[1], na_recv.at[1], mate, e))

    def ag_copy(j):
        return rc(AG.at[mj], AG.at[mj], ag_send.at[j], ag_recv.at[mj], member(j), e)

    def agy_copy():
        return rc(AG.at[mj], AG.at[mj], one_send.at[1], ag_recv.at[mj], far, e)

    def ag_start():
        def go(j):
            @pl.when(j != z)
            def _():
                ag_copy(j).start()
        loop(8, go)

    def half_copy():
        half = pl.ds(8 * c, 8)
        return rc(AG.at[half], AG.at[half], one_send.at[5], one_recv.at[5], mate, e)

    def outer_half():
        def ag_wait(j):
            @pl.when(j != z)
            def _():
                got = c * 8 + j
                rc(AG.at[got], AG.at[got], ag_send.at[j], ag_recv.at[got], r, e).wait_recv()
        loop(8, ag_wait)
        half_copy().start()

    def nesterov(a, m, tot):
        delta = a - tot * (1.0 / 32.0)
        nm = OUTER_MOMENTUM * m + delta
        return a - OUTER_RATE * (delta + OUTER_MOMENTUM * nm), nm

    def outer_own():
        @pl.when(owner)
        def _():
            for copy in am_copies():
                copy.wait_recv()
            ps_copy().wait_recv()
            TOT[...] += PSR[...].astype(F32)
            mine = pl.ds(pl.multiple_of(8 * c, 8), 8)
            other = pl.ds(pl.multiple_of(8 - 8 * c, 8), 8)
            na, nm = nesterov(anc[...], mom[...], TOT[mine, :])
            out_anc[...] = na
            out_mom[...] = nm
            nb, nn = nesterov(ANCR[...], MOMR[...], TOT[other, :])
            NAS[...] = nb
            NMS[...] = nn
            for copy in na_copies():
                copy.start()
            TOT[mine, :] = na
            TOT[other, :] = nb
            AG[mj] = TOT[...].astype(BF16)
            agy_copy().start()
            ag_start()

    def outer_pass():
        @pl.when(c != yh)
        def _():
            agy_copy().wait_recv()
            ag_start()

    def arrived(p, slot):
        rc(R.at[p, slot, win], R.at[p, slot, win], gu_send.at[p, slot], r_recv.at[p, slot], r, e).wait_recv()

    def to_partner(p, s):
        slot = s * 4 + x
        return rc(T.at[p, s, win], R.at[p, slot, win], xp_send.at[p, s], r_recv.at[p, slot], r, px * 4 + y)

    def to_cross(p, s):
        slot = s * 4 + x
        return rc(T.at[p, s, wot], R.at[p, slot, wot], xc_send.at[p, s], r_recv.at[p, slot], r, cx * 4 + y)

    def on_to_partner(p, s):
        slot = s * 4 + cx
        return rc(R.at[p, slot, win], R.at[p, slot, win], xf_send.at[p, s], r_recv.at[p, slot], r, px * 4 + y)

    def own_copy(p, s):
        slot = s * 4 + x
        return pltpu.make_async_copy(T.at[p, s, win], R.at[p, slot, win], r_recv.at[p, slot])

    def to_guest(p, slot):
        return rc(R.at[p, slot, win], R.at[p, slot, win], gu_send.at[p, slot], r_recv.at[p, slot], mate, e)

    def own_to_guest(p, s):
        slot = s * 4 + x
        return rc(T.at[p, s, win], R.at[p, slot, win], gu_send.at[p, slot], r_recv.at[p, slot], mate, e)

    @pl.when(home)
    def _():
        for p in (0, 1):
            to_partner(p, y).start()
            to_cross(p, y).start()

    ch_copy().start()

    @pl.when(c != yh)
    def _():
        for copy in am_copies():
            copy.start()

    loop(8, g_start)

    @pl.when(home)
    def _():
        GROW[myslot] = GSRC[x // 2]

    for p in range(4):
        R[p, :, fill, :] = jnp.zeros((16, 32, HALF), BF16)

    def hidden(s, units):
        rows0 = R[0, pl.ds(s * 4, 4)].reshape(512, HALF)
        rows1 = R[1, pl.ds(s * 4, 4)].reshape(512, HALF)
        for n in range(units):
            au = (jnp.dot(rows0, WU[n, :HALF, :], preferred_element_type=F32)
                  + jnp.dot(rows1, WU[n, HALF:, :], preferred_element_type=F32))
            a = au[:, :128]
            H[s, :, 128 * n:128 * (n + 1)] = (a / (1.0 + jnp.exp(-a)) * au[:, 128:]).astype(BF16)

    def grads(s, half, units):
        rows = R[2 + half, pl.ds(s * 4, 4)].reshape(512, HALF)
        cols = [jnp.sum(eye * GROW[s * 4 + j], axis=1, keepdims=True) for j in range(4)]
        hg = jnp.transpose((H[s, :, :128 * units].astype(F32) * jnp.concatenate(cols, axis=0)).astype(BF16))
        for d, w in ((0, 256), (256, 256), (512, 384)):
            at = slice(HALF * half + d, HALF * half + d + w)
            ACC[:128 * units, at] += jnp.dot(hg, rows[:, d:d + w], preferred_element_type=F32)

    def router(s, half, units):
        rows = R[2 + half, pl.ds(s * 4, 4)].reshape(512, HALF)
        down_rows = WD[:units, :, HALF * half:HALF * (half + 1)].reshape(128 * units, HALF)
        proj = lax.dot_general(rows, down_rows, NT, preferred_element_type=F32)
        qcol = jnp.sum(H[s, :, :128 * units].astype(F32) * proj, axis=1, keepdims=True)
        for j in range(4):
            Q[s * 4 + j] += jnp.sum(eye * qcol[j * 128:(j + 1) * 128], axis=0, keepdims=True)

    ACC[...] = jnp.zeros((384, D), F32)
    Q[...] = jnp.zeros((16, 1, 128), F32)

    def gg_copy():
        return rc(GROW, GROW, one_send.at[2], one_recv.at[2], mate, e)

    def qg_copy():
        return rc(Q, QG, one_send.at[3], one_recv.at[3], mate, e)

    def gr_out(half):
        GSND[half] = (scale * ACC[:, HALF * half:HALF * (half + 1)]).astype(BF16)

    def gr_to(half, kind, src, count, dst, exp):
        return rc(GSND.at[half, pl.ds(src, count)], GRCV.at[half, pl.ds(dst, count)], gr_send.at[half, kind],
                  gr_recv.at[half, kind], mate, exp)

    def gr_edge(half):
        return gr_to(half, 0, 0, 128, 0, peer_e)

    def gr_mid(half):
        return gr_to(half, 0, 0, 256, 0, peer_e), gr_to(half, 1, 256, 128, 128, other_e)

    def w_unit(src, dst, exp):
        cols = pl.ds(128 * src, 128)
        up_gate = (rc(wg.at[:, cols], WU.at[dst, :, pl.ds(0, 128)], w_send.at[dst, 0], w_recv.at[dst, 0], mate, exp),
                   rc(wu.at[:, cols], WU.at[dst, :, pl.ds(128, 128)], w_send.at[dst, 1], w_recv.at[dst, 1], mate, exp))
        return up_gate, rc(wd.at[cols, :], WD.at[dst], w_send.at[dst, 2], w_recv.at[dst, 2], mate, exp)

    def w_start(pair):
        for copy in pair:
            copy.start()

    def w_sent(pair):
        for copy in pair:
            copy.wait_send()

    def w_arrived(units):
        for n in range(units):
            for copy in w_unit(0, n, e)[0]:
                copy.wait_recv()

    def q_copy(slot):
        return rc(Q.at[slot], QR.at[x * 2 + y // 2], q_send.at[slot], q_recv.at[x * 2 + y // 2],
                  r, (slot % 4) * 4 + slot // 4)

    def drain(i):
        p, s = i // 4, i % 4

        @pl.when(home | (mid & (s != y)))
        def _():
            line_drain(p, s)

        @pl.when(guest & mid & (s == y) & (p > 1))
        def _():
            line_drain(p, s)

        @pl.when(home)
        def _():
            to_partner(p, s).wait_send()
            to_cross(p, s).wait_send()
            on_to_partner(p, s).wait_send()
            for col in range(4):
                to_guest(p, s * 4 + col).wait_send()

    def drain_z(j):
        @pl.when(j != z)
        def _():
            rs_copy(j).wait_send()
            ag_copy(j).wait_send()
    def drain_g(j):
        @pl.when(home_of(j) != e)
        def _():
            g_copy(j).wait_send()

    def drains():
        loop(16, drain)
        loop(8, drain_z)
        loop(8, drain_g)

    def merge(j, grad):
        rows = pl.ds(pl.multiple_of(16 * j, 16), 16)
        for half in (0, 1):
            cols = pl.ds(HALF * half, HALF)
            out_frag[rows, cols] = (MIX * Wo[rows, cols].astype(F32) - MIX * INNER_RATE * grad(rows, half)
                                    + (1.0 - MIX) * AG[j, :, cols].astype(F32)).astype(BF16)

    def guest_work(units):
        w_arrived(units)
        gg_copy().wait_recv()

        def step(i):
            if units == 3:
                for n in (13, 14, 15):
                    @pl.when(i == 4 * n - 48)
                    def _(n=n):
                        line_step(*item(n))

                @pl.when(i == 10)
                def _():
                    outer_half()

            p, s = item(i)
            for col in (x, cx, px, ox):
                arrived(p, s * 4 + col)

            @pl.when(p == 1)
            def _():
                hidden(s, units)

            for half in (0, 1):
                @pl.when(p == 2 + half)
                def _():
                    grads(s, half, units)

            @pl.when(i == 12)
            def _():
                gr_out(0)
                for copy in ((gr_edge(0),) if units == 1 else gr_mid(0)):
                    copy.start()
                for n in range(units):
                    w_unit(0, n, e)[1].wait_recv()
                loop(4, lambda k: router(k, 0, units))
                router(y, 1, units)

            @pl.when(i == 15)
            def _():
                gr_out(1)
                for copy in ((gr_edge(1),) if units == 1 else gr_mid(1)):
                    copy.start()

            @pl.when(i > 12)
            def _():
                router(s, 1, units)
        loop(16, step)
        qg_copy().start()

    @pl.when(home)
    def _():
        def g_wait(slot):
            @pl.when(slot != myslot)
            def _():
                rc(GROW.at[slot], GROW.at[slot], g_send.at[0], g_recv.at[slot], r, e).wait_recv()

        def step(i):
            @pl.when(i < 16)
            def _():
                p, s = item(i)
                own_to_guest(p, s).start()
                own_copy(p, s).start()

            @pl.when((i > 0) & (i < 17))
            def _():
                p, s = item(i - 1)
                arrived(p, s * 4 + cx)
                on_to_partner(p, s).start()
                to_guest(p, s * 4 + cx).start()
                arrived(p, s * 4 + px)
                to_guest(p, s * 4 + px).start()

            @pl.when(i == 1)
            def _():
                outer_start()

            @pl.when(i == 2)
            def _():
                line_send(2, y)

            @pl.when(i == 4)
            def _():
                line_send(3, y)

            @pl.when((i > 2) & (i < 15))
            def _():
                line_step(*item(i + 1))

            @pl.when((i > 0) & (i < 15))
            def _():
                p, s = item(i + 1)
                to_partner(p, s).start()
                to_cross(p, s).start()

            @pl.when(i == 2)
            def _():
                for copy in w_local():
                    copy.wait()

            @pl.when(i == 3)
            def _():
                loop(16, g_wait)
                gg_copy().start()

            @pl.when(i > 1)
            def _():
                p, s = item(i - 2)
                arrived(p, s * 4 + ox)
                to_guest(p, s * 4 + ox).start()
                own_copy(p, s).wait()

                @pl.when(p == 1)
                def _():
                    hidden(s, 2)

                for half in (0, 1):
                    @pl.when(p == 2 + half)
                    def _():
                        grads(s, half, 2)
                        router(s, half, 2)

            @pl.when(i == 5)
            def _():
                outer_sum()

            @pl.when(i == 8)
            def _():
                outer_own()

            @pl.when(i == 10)
            def _():
                outer_pass()

            @pl.when(i == 15)
            def _():
                outer_half()
        loop(18, step)

        drains()
        half_copy().wait_recv()
        loop(16, lambda j: merge(j, lambda rows, half: scale * ACC[rows, HALF * half:HALF * (half + 1)]))
        qg_copy().wait_recv()
        Q[...] += QG[...]

        def q_start(slot):
            @pl.when(slot != myslot)
            def _():
                q_copy(slot).start()
        loop(16, q_start)
        QR[x * 2 + y // 2] = Q[myslot]

    @pl.when(guest)
    def _():
        outer_start()
        for p in (0, 1):
            line_drain(p, y)
            line_send(p + 2, y)

    @pl.when(guest & edge)
    def _():
        for p in (2, 3):
            line_drain(p, y)
        units = [w_unit(n, n, peer_e) for n in (0, 1)]
        w_start(units[0][0])
        w_start(units[1][0])
        outer_sum()
        w_sent(units[0][0])
        w_sent(units[1][0])
        units[0][1].start()
        units[1][1].start()
        outer_own()
        outer_pass()
        outer_half()
        guest_work(1)

    @pl.when(guest & mid)
    def _():
        to_edge = w_unit(0, 0, peer_e)
        to_mid = w_unit(1, 2, other_e)
        for i in range(4, 13):
            if i == 6:
                w_start(to_edge[0])
                w_start(to_mid[0])
            if i == 7:
                outer_sum()
            if i == 9:
                outer_own()
            if i == 11:
                outer_pass()
            line_step(*item(i))
        w_sent(to_edge[0])
        to_edge[1].start()
        w_sent(to_mid[0])
        to_mid[1].start()
        guest_work(3)

    @pl.when(guest)
    def _():
        drains()
        half_copy().wait_recv()

    @pl.when(guest & edge)
    def _():
        for half in (0, 1):
            gr_to(half, 0, 0, 256, 0, e).wait_recv()

    @pl.when(guest & mid)
    def _():
        for half in (0, 1):
            gr_to(half, 0, 0, 128, 0, e).wait_recv()
            gr_to(half, 1, 0, 128, 128, e).wait_recv()

    @pl.when(guest)
    def _():
        loop(16, lambda j: merge(j, lambda rows, half: GRCV[half, rows].astype(F32)))

    @pl.when(c != yh)
    def _():
        for copy in na_copies():
            copy.wait_recv()
        out_anc[...] = NAR[...]
        out_mom[...] = NMR[...]

    def q_wait(j):
        @pl.when(home_of(j) != e)
        def _():
            rc(QR.at[j], QR.at[j], q_send.at[0], q_recv.at[j], r, e).wait_recv()
    loop(8, q_wait)
    q0 = QR[0] + QR[1] + QR[2] + QR[3]
    q1 = QR[4] + QR[5] + QR[6] + QR[7]
    picked = PT[...] * (ebc * q1 + (1.0 - ebc) * q0)
    out_gate[...] = scale * jnp.sum(eye * jnp.sum(picked, axis=1, keepdims=True), axis=0, keepdims=True)

    def drain_small(j):
        @pl.when(home & (j != myslot))
        def _():
            q_copy(j).wait_send()
    loop(16, drain_small)

    ch_copy().wait_send()
    half_copy().wait_send()

    @pl.when(home)
    def _():
        gg_copy().wait_send()

    @pl.when(guest)
    def _():
        qg_copy().wait_send()

    @pl.when(guest & edge)
    def _():
        for n in (0, 1):
            w_unit(n, n, peer_e)[1].wait_send()
        for half in (0, 1):
            gr_edge(half).wait_send()

    @pl.when(guest & mid)
    def _():
        w_unit(0, 0, peer_e)[1].wait_send()
        w_unit(1, 2, other_e)[1].wait_send()
        for half in (0, 1):
            for copy in gr_mid(half):
                copy.wait_send()

    @pl.when(owner)
    def _():
        agy_copy().wait_send()
        for copy in na_copies():
            copy.wait_send()

    @pl.when(c != yh)
    def _():
        ps_copy().wait_send()
        for copy in am_copies():
            copy.wait_send()


def handover(a, b, c, d, a2, b2, c2, d2):
    a2[...] = a[...]
    b2[...] = b[...]
    c2[...] = c[...]
    d2[...] = d[...]


def per_device(tokens, cotangent, expert_ids, gate_values, w_gate, w_up, w_down, anchor, momentum):
    D = tokens.shape[1]
    vm = pl.BlockSpec(memory_space=pltpu.VMEM)
    dma = pltpu.SemaphoreType.DMA
    V = pltpu.VMEM
    gate, frag, anc, mom = pl.pallas_call(
        kernel,
        out_shape=(
            jax.ShapeDtypeStruct((1, 128), F32),
            jax.ShapeDtypeStruct((256, D), BF16),
            jax.ShapeDtypeStruct((8, D), F32),
            jax.ShapeDtypeStruct((8, D), F32),
        ),
        in_specs=[vm] * 4 + [pl.BlockSpec(memory_space=pl.ANY)] * 3 + [vm] * 2,
        out_specs=[vm] * 4,
        scratch_shapes=[
            V((4, 16, 128, D // 2), BF16), V((4, 4, 128, D // 2), BF16),
            V((3, D, 256), BF16), V((3, 128, D), BF16), V((256, D), BF16),
            V((4, 512, 384), BF16), V((384, D), F32), V((2, 384, D // 2), BF16), V((2, 256, D // 2), BF16), V((128, 128), F32),
            V((128, D), BF16), V((8, 16, D), BF16), V((8, 16, D), BF16), V((16, D), F32), V((16, D), BF16), V((16, D), BF16), V((16, 16, D), BF16),
            V((8, D), F32), V((8, D), F32), V((8, D), F32), V((8, D), F32), V((8, D), F32), V((8, D), F32),
            V((2, 1, 128), F32), V((16, 1, 128), F32), V((16, 1, 128), F32), V((16, 1, 128), F32), V((8, 1, 128), F32),
            dma((4, 4)), dma((4, 4)), dma((4, 4)), dma((4, 16)), dma((4, 4)), dma((4, 4)), dma((4, 4)), dma((4, 16)),
            dma((3, 3)), dma((3, 3)),
            dma((8,)), dma((16,)), dma((16,)), dma((8,)), dma((16,)), dma((16,)), dma((16,)), dma((16,)),
            dma((2,)), dma((2,)), dma((2,)), dma((2,)), dma((6,)), dma((6,)), dma((8,)), dma((2, 2)), dma((2, 2)),
        ],
        compiler_params=pltpu.CompilerParams(
            collective_id=0, has_side_effects=True, vmem_limit_bytes=58 * 1024 * 1024),
        name="step",
    )(tokens, cotangent, expert_ids.reshape(1, 128), gate_values.reshape(1, 128), w_gate[0], w_up[0], w_down[0], anchor[0], momentum[0])
    gate, frag, anc, mom = pl.pallas_call(
        handover,
        out_shape=(
            jax.ShapeDtypeStruct((1, 128), F32),
            jax.ShapeDtypeStruct((256, D), BF16),
            jax.ShapeDtypeStruct((8, D), F32),
            jax.ShapeDtypeStruct((8, D), F32),
        ),
        in_specs=[vm] * 4,
        out_specs=[vm] * 4,
        compiler_params=pltpu.CompilerParams(vmem_limit_bytes=58 * 1024 * 1024),
        name="handover",
    )(gate, frag, anc, mom)
    return gate.reshape(128, 1), frag[None, None], anc[None], mom[None]


def solution(mesh):
    return jax.shard_map(
        per_device,
        mesh=mesh,
        in_specs=(
            P(("replica", "expert"), None),
            P(("replica", "expert"), None),
            P(("replica", "expert"), None),
            P(("replica", "expert"), None),
            P("replica", None, "expert"),
            P("replica", None, "expert"),
            P("replica", "expert", None),
            P("expert", "replica", None),
            P("expert", "replica", None),
        ),
        out_specs=(
            P(("replica", "expert"), None),
            P("replica", "expert", None, None),
            P("expert", "replica", None),
            P("expert", "replica", None),
        ),
        check_vma=False,
    )
```

```python
import math

import jax
import jax.numpy as jnp
from jax import lax
from jax.experimental import pallas as pl
from jax.experimental.pallas import tpu as pltpu
from jax.sharding import PartitionSpec as P

HID = 2048
OUTER_RATE = 0.7
OUTER_MOMENTUM = 0.9
MIX = 0.5
INNER_RATE = 8.0
WIN = 96
F32 = jnp.float32
BF16 = jnp.bfloat16
MESH = pl.DeviceIdType.MESH
NT = (((1,), (1,)), ((), ()))
TN = (((0,), (0,)), ((), ()))


def kernel(tok_in, cot_in, ids, gates, wg, wu, wd, anc, mom,
           out_gate, out_frag, out_anc, out_mom,
           tok, cot, R, T, WU, WD, Wo, H, ACC, GSND, GRCV, PT,
           CH, RSS, RS, TOT, PSS, PSR, AG, ANCR, MOMR, NAS, NMS, NAR, NMR,
           GSRC, GROW, Q, QG, QR,
           y_recv, y_up, y_dn, r_recv, xp_send, xc_send, xf_send, gu_send, w_send, w_recv,
           g_send, g_recv, q_send, q_recv, rs_send, rs_recv, ag_send, ag_recv,
           am_send, am_recv, na_send, na_recv, one_send, one_recv, l_sem, gr_send, gr_recv):
    D = tok.shape[1]
    HALF = D // 2
    scale = 1.0 / math.sqrt(HID)
    r = lax.axis_index("replica")
    e = lax.axis_index("expert")
    c = r % 2
    z = (r // 2) % 8
    yh = r // 16
    x = e // 4
    y = e % 4
    home = (c + y) % 2 == 0
    guest = (c + y) % 2 == 1
    owner = c == yh
    mid = (y == 1) | (y == 2)
    edge = (y == 0) | (y == 3)
    other_e = e - 2 * y + 3
    mate = r + 1 - 2 * c
    peer_e = e + 1 - 2 * (e % 2)
    far = r + 16 - 32 * yh
    px = x + 1 - 2 * (x % 2)
    cx = 3 - x
    ox = 3 - px
    w0 = pl.multiple_of(32 * (x // 2), 32)
    win = pl.ds(w0, WIN)
    wot = pl.ds(pl.multiple_of(32 - 32 * (x // 2), 32), WIN)
    fill = pl.ds(pl.multiple_of(96 - 96 * (x // 2), 32), 32)
    mj = c * 8 + z
    myslot = y * 4 + x
    yu = y // 2
    yy = y + yu * (3 - 2 * y)

    def rc(src, dst, ss, rs, rep, exp):
        return pltpu.make_async_remote_copy(
            src_ref=src, dst_ref=dst, send_sem=ss, recv_sem=rs, device_id=(rep, exp), device_id_type=MESH)

    def item(i):
        ge4, ge13 = (i + 12) // 16, (i + 3) // 16
        k = ge4 * (1 - ge13) * ((i + 11) // 3 - 4) + ge13 * (i - 12)
        p = (1 - ge4) * i + ge4 * (1 - ge13) * ((i + 11) % 3) + ge13 * 3
        kk = k // 2
        f = (1 - kk) * (yy + k * (1 - 2 * yy)) + kk * k
        return p, f + yu * (3 - 2 * f)

    def member(j):
        return yh * 16 + j * 2 + c

    def loop(n, body):
        def step(i, carry):
            body(i)
            return carry
        lax.fori_loop(0, n, step, 0)

    own = pltpu.make_async_copy(wd, Wo, l_sem.at[0])
    own.start()
    rows_in = [pltpu.make_async_copy(a, b, l_sem.at[8 + n]) for n, (a, b) in enumerate(((tok_in, tok), (cot_in, cot)))]
    for copy in rows_in:
        copy.start()

    def w_local():
        pairs = []
        for n in (0, 1):
            cols = pl.ds(128 * n, 128)
            pairs += [(wg.at[:, cols], WU.at[n, :, pl.ds(0, 128)]), (wu.at[:, cols], WU.at[n, :, pl.ds(128, 128)]),
                      (wd.at[cols, :], WD.at[n])]
        return [pltpu.make_async_copy(a, b, l_sem.at[2 + n]) for n, (a, b) in enumerate(pairs)]

    @pl.when(home)
    def _():
        for copy in w_local():
            copy.start()

    bar = pltpu.get_barrier_semaphore()

    def hello(j):
        @pl.when(j != e)
        def _():
            pl.semaphore_signal(bar, inc=1, device_id=(r, j), device_id_type=MESH)

    loop(16, hello)

    def hello_z(j):
        @pl.when(j != z)
        def _():
            pl.semaphore_signal(bar, inc=1, device_id=(member(j), e), device_id_type=MESH)
    loop(8, hello_z)
    pl.semaphore_signal(bar, inc=1, device_id=(mate, e), device_id_type=MESH)
    pl.semaphore_signal(bar, inc=1, device_id=(mate, peer_e), device_id_type=MESH)
    pl.semaphore_signal(bar, inc=1, device_id=(far, e), device_id_type=MESH)

    @pl.when(mid)
    def _():
        pl.semaphore_signal(bar, inc=1, device_id=(mate, other_e), device_id_type=MESH)

    rowi = lax.broadcasted_iota(jnp.int32, (128, 128), 0)
    lane = lax.broadcasted_iota(jnp.int32, (128, 128), 1)
    eye = (rowi == lane).astype(F32)
    ecol = jnp.sum(eye * ids[...].astype(F32), axis=1, keepdims=True)
    gcol = jnp.sum(eye * gates[...].astype(F32), axis=1, keepdims=True)
    ebc = jnp.broadcast_to(ecol, (128, 128))
    lower = (lane < rowi).astype(BF16)
    ones = jnp.ones((128, 128), BF16)
    ebf = ebc.astype(BF16)
    before = jnp.dot(lower, ebf, preferred_element_type=F32)
    total1 = jnp.dot(ones, ebf, preferred_element_type=F32)
    pos = ebc * (128.0 - total1 + before) + (1.0 - ebc) * (rowi.astype(F32) - before)
    perm = (pos == lane.astype(F32)).astype(F32)
    PT[...] = perm
    permb = jnp.transpose(perm).astype(BF16)
    for copy in rows_in:
        copy.wait()
    for p, rows in enumerate((tok, tok, cot, cot)):
        cols = pl.ds(HALF * (p % 2), HALF)
        part = jnp.dot(permb, rows[:, cols], preferred_element_type=F32).astype(BF16)

        @pl.when(home)
        def _(p=p, part=part):
            R[p, myslot] = part

        @pl.when(guest)
        def _(p=p, part=part):
            T[p, y] = part
    gp = perm * gcol
    g1 = jnp.sum(gp * ebc, axis=0, keepdims=True)
    g0 = jnp.sum(gp * (1.0 - ebc), axis=0, keepdims=True)
    GSRC[0] = g0
    GSRC[1] = g1

    pl.semaphore_wait(bar, 25 + y * (3 - y) // 2)

    def up(p, s, at_home):
        a, b = R.at[p, s * 4 + x], T.at[p, s]
        return rc(a if at_home else b, b if at_home else a, y_up.at[p, s], y_recv.at[p, s], r, e + 1)

    def down(p, s, at_home):
        a, b = R.at[p, s * 4 + x], T.at[p, s]
        return rc(a if at_home else b, b if at_home else a, y_dn.at[p, s], y_recv.at[p, s], r, e - 1)

    def line_send(p, s, at_home):
        @pl.when((s <= y) & (y < 2 + c))
        def _():
            up(p, s, at_home).start()

        @pl.when((s >= y) & (y > c))
        def _():
            down(p, s, at_home).start()

    def line_drain(p, s, at_home):
        @pl.when((s <= y) & (y < 2 + c))
        def _():
            up(p, s, at_home).wait_send()

        @pl.when((s >= y) & (y > c))
        def _():
            down(p, s, at_home).wait_send()

    def line_step(p, s, at_home):
        @pl.when(((s < y) & (y <= 2 + c)) | ((s > y) & (y >= c)))
        def _():
            got = R.at[p, s * 4 + x] if at_home else T.at[p, s]
            rc(got, got, y_up.at[p, s], y_recv.at[p, s], r, e).wait_recv()
        line_send(p, s, at_home)

    @pl.when(guest)
    def _():
        line_send(0, y, False)
        line_send(1, y, False)

    @pl.when(home)
    def _():
        line_send(0, y, True)
        line_send(1, y, True)

    def ch_copy():
        return rc(wd.at[pl.ds(pl.multiple_of(128 - 128 * c, 128), 128), :], CH, one_send.at[4], one_recv.at[4], mate, e)

    def rs_copy(j):
        return rc(RSS.at[j], RS.at[z], rs_send.at[j], rs_recv.at[z], member(j), e)

    def outer_start():
        own.wait()
        ch_copy().wait_recv()

        def pair(j):
            rows = pl.ds(pl.multiple_of(16 * j, 16), 16)
            mine = Wo[pl.ds(pl.multiple_of(128 * c + 16 * j, 16), 16), :]
            RSS[j] = (mine.astype(F32) + CH[rows, :].astype(F32)).astype(BF16)
        loop(8, pair)
        RS[z] = RSS[z]

        def rs_start(j):
            @pl.when(j != z)
            def _():
                rs_copy(j).start()
        loop(8, rs_start)

    def am_copies():
        return (rc(anc, ANCR, am_send.at[0], am_recv.at[0], mate, e),
                rc(mom, MOMR, am_send.at[1], am_recv.at[1], mate, e))

    def home_of(j):
        return (j // 2) * 4 + c + 2 * (j % 2)

    def g_copy(j):
        return rc(GSRC.at[j // 4], GROW.at[myslot], g_send.at[j], g_recv.at[myslot], r, home_of(j))

    def g_start(j):
        @pl.when(home_of(j) != e)
        def _():
            g_copy(j).start()
    def ps_copy():
        return rc(PSS, PSR, one_send.at[0], one_recv.at[0], far, e)

    def outer_sum():
        def rs_wait(j):
            @pl.when(j != z)
            def _():
                rc(RS.at[j], RS.at[j], rs_send.at[j], rs_recv.at[j], r, e).wait_recv()
        loop(8, rs_wait)
        TOT[...] = jnp.zeros((16, D), F32)

        def rs_add(j):
            TOT[...] += RS[j].astype(F32)
        loop(8, rs_add)

        @pl.when(c != yh)
        def _():
            PSS[...] = TOT[...].astype(BF16)
            ps_copy().start()

    def na_copies():
        return (rc(NAS, NAR, na_send.at[0], na_recv.at[0], mate, e),
                rc(NMS, NMR, na_send.at[1], na_recv.at[1], mate, e))

    def ag_copy(j):
        return rc(AG.at[mj], AG.at[mj], ag_send.at[j], ag_recv.at[mj], member(j), e)

    def agy_copy():
        return rc(AG.at[mj], AG.at[mj], one_send.at[1], ag_recv.at[mj], far, e)

    def ag_start():
        def go(j):
            @pl.when(j != z)
            def _():
                ag_copy(j).start()
        loop(8, go)

    def half_copy():
        half = pl.ds(8 * c, 8)
        return rc(AG.at[half], AG.at[half], one_send.at[5], one_recv.at[5], mate, e)

    def outer_half():
        def ag_wait(j):
            @pl.when(j != z)
            def _():
                got = c * 8 + j
                rc(AG.at[got], AG.at[got], ag_send.at[j], ag_recv.at[got], r, e).wait_recv()
        loop(8, ag_wait)
        half_copy().start()

    def nesterov(a, m, tot):
        delta = a - tot * (1.0 / 32.0)
        nm = OUTER_MOMENTUM * m + delta
        return a - OUTER_RATE * (delta + OUTER_MOMENTUM * nm), nm

    def outer_own():
        @pl.when(owner)
        def _():
            for copy in am_copies():
                copy.wait_recv()
            ps_copy().wait_recv()
            TOT[...] += PSR[...].astype(F32)
            mine = pl.ds(pl.multiple_of(8 * c, 8), 8)
            other = pl.ds(pl.multiple_of(8 - 8 * c, 8), 8)
            na, nm = nesterov(anc[...], mom[...], TOT[mine, :])
            out_anc[...] = na
            out_mom[...] = nm
            nb, nn = nesterov(ANCR[...], MOMR[...], TOT[other, :])
            NAS[...] = nb
            NMS[...] = nn
            for copy in na_copies():
                copy.start()
            TOT[mine, :] = na
            TOT[other, :] = nb
            AG[mj] = TOT[...].astype(BF16)
            agy_copy().start()
            ag_start()

    def outer_pass():
        @pl.when(c != yh)
        def _():
            agy_copy().wait_recv()
            ag_start()

    def arrived(p, slot):
        rc(R.at[p, slot, win], R.at[p, slot, win], gu_send.at[p, slot], r_recv.at[p, slot], r, e).wait_recv()

    def to_partner(p, s):
        slot = s * 4 + x
        return rc(R.at[p, slot, win], R.at[p, slot, win], xp_send.at[p, s], r_recv.at[p, slot], r, px * 4 + y)

    def to_cross(p, s):
        slot = s * 4 + x
        return rc(R.at[p, slot, wot], R.at[p, slot, wot], xc_send.at[p, s], r_recv.at[p, slot], r, cx * 4 + y)

    def on_to_partner(p, s):
        slot = s * 4 + cx
        return rc(R.at[p, slot, win], R.at[p, slot, win], xf_send.at[p, s], r_recv.at[p, slot], r, px * 4 + y)

    def to_guest(p, s):
        rows = R.at[p, pl.ds(s * 4, 4), win]
        return rc(rows, rows, gu_send.at[p, s], r_recv.at[p, s * 4], mate, e)

    @pl.when(home)
    def _():
        for p in (0, 1):
            to_partner(p, y).start()
            to_cross(p, y).start()

    ch_copy().start()

    @pl.when(c != yh)
    def _():
        for copy in am_copies():
            copy.start()

    loop(8, g_start)

    @pl.when(home)
    def _():
        GROW[myslot] = GSRC[x // 2]

    for p in range(4):
        for k in range(4):
            for d in (1, 2, 3):
                R[p, 4 * k + (x + d) % 4, fill, :] = jnp.zeros((32, HALF), BF16)

    @pl.when(guest)
    def _():
        for p in range(4):
            for k in range(4):
                R[p, 4 * k + x, fill, :] = jnp.zeros((32, HALF), BF16)

    def hidden(s, units):
        rows0 = R[0, pl.ds(s * 4, 4)].reshape(512, HALF)
        rows1 = R[1, pl.ds(s * 4, 4)].reshape(512, HALF)
        for n in range(units):
            au = (jnp.dot(rows0, WU[n, :HALF, :], preferred_element_type=F32)
                  + jnp.dot(rows1, WU[n, HALF:, :], preferred_element_type=F32))
            a = au[:, :128]
            H[s, :, 128 * n:128 * (n + 1)] = (a / (1.0 + jnp.exp(-a)) * au[:, 128:]).astype(BF16)

    def grads(s, half, units):
        rows = R[2 + half, pl.ds(s * 4, 4)].reshape(512, HALF)
        cols = [jnp.sum(eye * GROW[s * 4 + j], axis=1, keepdims=True) for j in range(4)]
        hg = jnp.transpose((H[s, :, :128 * units].astype(F32) * jnp.concatenate(cols, axis=0)).astype(BF16))
        for d, w in ((0, 256), (256, 256), (512, 384)):
            at = slice(HALF * half + d, HALF * half + d + w)
            ACC[:128 * units, at] += jnp.dot(hg, rows[:, d:d + w], preferred_element_type=F32)

    def router(s, half, units):
        rows = R[2 + half, pl.ds(s * 4, 4)].reshape(512, HALF)
        down_rows = WD[:units, :, HALF * half:HALF * (half + 1)].reshape(128 * units, HALF)
        proj = lax.dot_general(rows, down_rows, NT, preferred_element_type=F32)
        qcol = jnp.sum(H[s, :, :128 * units].astype(F32) * proj, axis=1, keepdims=True)
        for j in range(4):
            Q[s * 4 + j] += jnp.sum(eye * qcol[j * 128:(j + 1) * 128], axis=0, keepdims=True)

    ACC[...] = jnp.zeros((384, D), F32)
    Q[...] = jnp.zeros((16, 1, 128), F32)

    def gg_copy():
        return rc(GROW, GROW, one_send.at[2], one_recv.at[2], mate, e)

    def qg_copy():
        return rc(Q, QG, one_send.at[3], one_recv.at[3], mate, e)

    def gr_out(half):
        GSND[half] = (scale * ACC[:, HALF * half:HALF * (half + 1)]).astype(BF16)

    def gr_to(half, kind, src, count, dst, exp):
        return rc(GSND.at[half, pl.ds(src, count)], GRCV.at[half, pl.ds(dst, count)], gr_send.at[half, kind],
                  gr_recv.at[half, kind], mate, exp)

    def gr_edge(half):
        return gr_to(half, 0, 0, 128, 0, peer_e)

    def gr_mid(half):
        return gr_to(half, 0, 0, 256, 0, peer_e), gr_to(half, 1, 256, 128, 128, other_e)

    def w_unit(src, dst, exp):
        cols = pl.ds(128 * src, 128)
        up_gate = (rc(wg.at[:, cols], WU.at[dst, :, pl.ds(0, 128)], w_send.at[dst, 0], w_recv.at[dst, 0], mate, exp),
                   rc(wu.at[:, cols], WU.at[dst, :, pl.ds(128, 128)], w_send.at[dst, 1], w_recv.at[dst, 1], mate, exp))
        return up_gate, rc(wd.at[cols, :], WD.at[dst], w_send.at[dst, 2], w_recv.at[dst, 2], mate, exp)

    def w_start(pair):
        for copy in pair:
            copy.start()

    def w_sent(pair):
        for copy in pair:
            copy.wait_send()

    def w_arrived(units):
        for n in range(units):
            for copy in w_unit(0, n, e)[0]:
                copy.wait_recv()

    def q_copy(slot):
        return rc(Q.at[slot], QR.at[x * 2 + y // 2], q_send.at[slot], q_recv.at[x * 2 + y // 2],
                  r, (slot % 4) * 4 + slot // 4)

    def drain(i, at_home):
        p, s = i // 4, i % 4
        if at_home:
            line_drain(p, s, True)
            to_partner(p, s).wait_send()
            to_cross(p, s).wait_send()
            on_to_partner(p, s).wait_send()
            to_guest(p, s).wait_send()
        else:
            @pl.when(mid & ((s != y) | (p >= 2)))
            def _():
                line_drain(p, s, False)

    def drain_z(j):
        @pl.when(j != z)
        def _():
            rs_copy(j).wait_send()
            ag_copy(j).wait_send()
    def drain_g(j):
        @pl.when(home_of(j) != e)
        def _():
            g_copy(j).wait_send()

    def drains(at_home):
        loop(16, lambda i: drain(i, at_home))
        loop(8, drain_z)
        loop(8, drain_g)

    def merge(j, grad):
        rows = pl.ds(pl.multiple_of(16 * j, 16), 16)
        for half in (0, 1):
            cols = pl.ds(HALF * half, HALF)
            out_frag[rows, cols] = (MIX * Wo[rows, cols].astype(F32) - MIX * INNER_RATE * grad(rows, half)
                                    + (1.0 - MIX) * AG[j, :, cols].astype(F32)).astype(BF16)

    def guest_work(units):
        w_arrived(units)
        gg_copy().wait_recv()

        def step(i):
            if units == 3:
                for n in (13, 14, 15):
                    @pl.when(i == 4 * n - 48)
                    def _(n=n):
                        line_step(*item(n), False)

                @pl.when(i == 10)
                def _():
                    outer_half()

            p, s = item(i)
            to_guest(p, s).wait_recv()

            @pl.when(p == 1)
            def _():
                hidden(s, units)

            for half in (0, 1):
                @pl.when(p == 2 + half)
                def _():
                    grads(s, half, units)

            @pl.when(i == 12)
            def _():
                gr_out(0)
                for copy in ((gr_edge(0),) if units == 1 else gr_mid(0)):
                    copy.start()
                for n in range(units):
                    w_unit(0, n, e)[1].wait_recv()
                loop(4, lambda k: router(k, 0, units))
                router(y, 1, units)

            @pl.when(i == 15)
            def _():
                gr_out(1)
                for copy in ((gr_edge(1),) if units == 1 else gr_mid(1)):
                    copy.start()

            @pl.when(i > 12)
            def _():
                router(s, 1, units)
        loop(16, step)
        qg_copy().start()

    @pl.when(home)
    def _():
        def g_wait(slot):
            @pl.when(slot != myslot)
            def _():
                rc(GROW.at[slot], GROW.at[slot], g_send.at[0], g_recv.at[slot], r, e).wait_recv()

        def step(i):
            @pl.when((i > 0) & (i < 17))
            def _():
                p, s = item(i - 1)
                arrived(p, s * 4 + cx)
                on_to_partner(p, s).start()
                arrived(p, s * 4 + px)

            @pl.when(i == 1)
            def _():
                outer_start()

            @pl.when(i == 2)
            def _():
                line_send(2, y, True)

            @pl.when(i == 4)
            def _():
                line_send(3, y, True)

            @pl.when((i > 2) & (i < 15))
            def _():
                line_step(*item(i + 1), True)

            @pl.when((i > 0) & (i < 15))
            def _():
                p, s = item(i + 1)
                to_partner(p, s).start()
                to_cross(p, s).start()

            @pl.when(i == 2)
            def _():
                for copy in w_local():
                    copy.wait()

            @pl.when(i == 3)
            def _():
                loop(16, g_wait)
                gg_copy().start()

            @pl.when(i > 1)
            def _():
                p, s = item(i - 2)
                arrived(p, s * 4 + ox)
                to_guest(p, s).start()

                @pl.when(p == 1)
                def _():
                    hidden(s, 2)

                for half in (0, 1):
                    @pl.when(p == 2 + half)
                    def _():
                        grads(s, half, 2)
                        router(s, half, 2)

            @pl.when(i == 5)
            def _():
                outer_sum()

            @pl.when(i == 7)
            def _():
                outer_own()

            @pl.when(i == 9)
            def _():
                outer_pass()

            @pl.when(i == 13)
            def _():
                outer_half()
        loop(18, step)

        drains(True)
        half_copy().wait_recv()
        loop(16, lambda j: merge(j, lambda rows, half: scale * ACC[rows, HALF * half:HALF * (half + 1)]))
        qg_copy().wait_recv()
        Q[...] += QG[...]

        def q_start(slot):
            @pl.when(slot != myslot)
            def _():
                q_copy(slot).start()
        loop(16, q_start)
        QR[x * 2 + y // 2] = Q[myslot]

    @pl.when(guest)
    def _():
        outer_start()
        for p in (0, 1):
            line_drain(p, y, False)
            line_send(p + 2, y, False)

    @pl.when(guest & edge)
    def _():
        for p in (2, 3):
            line_drain(p, y, False)
        units = [w_unit(n, n, peer_e) for n in (0, 1)]
        chain = [*units[0][0], *units[1][0]]
        steps = (outer_sum, None, outer_own, outer_pass)
        for copy, then in zip(chain, steps):
            copy.start()
            if then is not None:
                then()
            copy.wait_send()
        units[0][1].start()
        units[1][1].start()
        outer_half()
        guest_work(1)

    @pl.when(guest & mid)
    def _():
        to_edge = w_unit(0, 0, peer_e)
        to_mid = w_unit(1, 2, other_e)
        for i in range(4, 13):
            if i == 6:
                w_start(to_edge[0])
                w_start(to_mid[0])
            if i == 7:
                outer_sum()
            if i == 9:
                outer_own()
            if i == 11:
                outer_pass()
            line_step(*item(i), False)
        w_sent(to_edge[0])
        to_edge[1].start()
        w_sent(to_mid[0])
        to_mid[1].start()
        guest_work(3)

    @pl.when(guest)
    def _():
        drains(False)
        half_copy().wait_recv()

    @pl.when(guest & edge)
    def _():
        for half in (0, 1):
            gr_to(half, 0, 0, 256, 0, e).wait_recv()

    @pl.when(guest & mid)
    def _():
        for half in (0, 1):
            gr_to(half, 0, 0, 128, 0, e).wait_recv()
            gr_to(half, 1, 0, 128, 128, e).wait_recv()

    @pl.when(guest)
    def _():
        loop(16, lambda j: merge(j, lambda rows, half: GRCV[half, rows].astype(F32)))

    @pl.when(c != yh)
    def _():
        for copy in na_copies():
            copy.wait_recv()
        out_anc[...] = NAR[...]
        out_mom[...] = NMR[...]

    def q_wait(j):
        @pl.when(home_of(j) != e)
        def _():
            rc(QR.at[j], QR.at[j], q_send.at[0], q_recv.at[j], r, e).wait_recv()
    loop(8, q_wait)
    q0 = QR[0] + QR[1] + QR[2] + QR[3]
    q1 = QR[4] + QR[5] + QR[6] + QR[7]
    picked = PT[...] * (ebc * q1 + (1.0 - ebc) * q0)
    out_gate[...] = scale * jnp.sum(eye * jnp.sum(picked, axis=1, keepdims=True), axis=0, keepdims=True)

    def drain_small(j):
        @pl.when(home & (j != myslot))
        def _():
            q_copy(j).wait_send()
    loop(16, drain_small)

    ch_copy().wait_send()
    half_copy().wait_send()

    @pl.when(home)
    def _():
        gg_copy().wait_send()

    @pl.when(guest)
    def _():
        qg_copy().wait_send()

    @pl.when(guest & edge)
    def _():
        for n in (0, 1):
            w_unit(n, n, peer_e)[1].wait_send()
        for half in (0, 1):
            gr_edge(half).wait_send()

    @pl.when(guest & mid)
    def _():
        w_unit(0, 0, peer_e)[1].wait_send()
        w_unit(1, 2, other_e)[1].wait_send()
        for half in (0, 1):
            for copy in gr_mid(half):
                copy.wait_send()

    @pl.when(owner)
    def _():
        agy_copy().wait_send()
        for copy in na_copies():
            copy.wait_send()

    @pl.when(c != yh)
    def _():
        ps_copy().wait_send()
        for copy in am_copies():
            copy.wait_send()


def handover(a, b, c, d, a2, b2, c2, d2):
    a2[...] = a[...]
    b2[...] = b[...]
    c2[...] = c[...]
    d2[...] = d[...]


def per_device(tokens, cotangent, expert_ids, gate_values, w_gate, w_up, w_down, anchor, momentum):
    D = tokens.shape[1]
    vm = pl.BlockSpec(memory_space=pltpu.VMEM)
    dma = pltpu.SemaphoreType.DMA
    V = pltpu.VMEM
    gate, frag, anc, mom = pl.pallas_call(
        kernel,
        out_shape=(
            jax.ShapeDtypeStruct((1, 128), F32),
            jax.ShapeDtypeStruct((256, D), BF16),
            jax.ShapeDtypeStruct((8, D), F32),
            jax.ShapeDtypeStruct((8, D), F32),
        ),
        in_specs=[pl.BlockSpec(memory_space=pl.ANY)] * 2 + [vm] * 2 + [pl.BlockSpec(memory_space=pl.ANY)] * 3 + [vm] * 2,
        out_specs=[vm] * 4,
        scratch_shapes=[
            V((128, D), BF16), V((128, D), BF16), V((4, 16, 128, D // 2), BF16), V((4, 4, 128, D // 2), BF16),
            V((3, D, 256), BF16), V((3, 128, D), BF16), V((256, D), BF16),
            V((4, 512, 384), BF16), V((384, D), F32), V((2, 384, D // 2), BF16), V((2, 256, D // 2), BF16), V((128, 128), F32),
            V((128, D), BF16), V((8, 16, D), BF16), V((8, 16, D), BF16), V((16, D), F32), V((16, D), BF16), V((16, D), BF16), V((16, 16, D), BF16),
            V((8, D), F32), V((8, D), F32), V((8, D), F32), V((8, D), F32), V((8, D), F32), V((8, D), F32),
            V((2, 1, 128), F32), V((16, 1, 128), F32), V((16, 1, 128), F32), V((16, 1, 128), F32), V((8, 1, 128), F32),
            dma((4, 4)), dma((4, 4)), dma((4, 4)), dma((4, 16)), dma((4, 4)), dma((4, 4)), dma((4, 4)), dma((4, 16)),
            dma((3, 3)), dma((3, 3)),
            dma((8,)), dma((16,)), dma((16,)), dma((8,)), dma((16,)), dma((16,)), dma((16,)), dma((16,)),
            dma((2,)), dma((2,)), dma((2,)), dma((2,)), dma((6,)), dma((6,)), dma((10,)), dma((2, 2)), dma((2, 2)),
        ],
        compiler_params=pltpu.CompilerParams(
            collective_id=0, has_side_effects=True, vmem_limit_bytes=58 * 1024 * 1024),
        name="step",
    )(tokens, cotangent, expert_ids.reshape(1, 128), gate_values.reshape(1, 128), w_gate[0], w_up[0], w_down[0], anchor[0], momentum[0])
    gate, frag, anc, mom = pl.pallas_call(
        handover,
        out_shape=(
            jax.ShapeDtypeStruct((1, 128), F32),
            jax.ShapeDtypeStruct((256, D), BF16),
            jax.ShapeDtypeStruct((8, D), F32),
            jax.ShapeDtypeStruct((8, D), F32),
        ),
        in_specs=[vm] * 4,
        out_specs=[vm] * 4,
        compiler_params=pltpu.CompilerParams(vmem_limit_bytes=58 * 1024 * 1024),
        name="handover",
    )(gate, frag, anc, mom)
    return gate.reshape(128, 1), frag[None, None], anc[None], mom[None]


def solution(mesh):
    return jax.shard_map(
        per_device,
        mesh=mesh,
        in_specs=(
            P(("replica", "expert"), None),
            P(("replica", "expert"), None),
            P(("replica", "expert"), None),
            P(("replica", "expert"), None),
            P("replica", None, "expert"),
            P("replica", None, "expert"),
            P("replica", "expert", None),
            P("expert", "replica", None),
            P("expert", "replica", None),
        ),
        out_specs=(
            P(("replica", "expert"), None),
            P("replica", "expert", None, None),
            P("expert", "replica", None),
            P("expert", "replica", None),
        ),
        check_vma=False,
    )
```
